32 devices in a mesh: grp: 2 (over x), chol: 16 (over z, y, core).
Axes of the slice: x: 2, y: 2, z: 4, core: 2. Of those that a mesh axis runs over, the one named last changes fastest.
Arguments:
- chol_vectors: bfloat16 [2048, 32768], P(None, 'chol'), may hold values from -0.03125 to 0.03125
- mean_greens: bfloat16 [32768], P('chol'), may hold values from -6 to 6
- greens: bfloat16 [512, 32768], P(('grp', 'chol')), parts along dimension 0, may hold values from -6 to 6
- walker_order: int32 [512], P('grp'), parts along dimension 0, may hold values from 0 to 255, each once
- noise_field: float32 [512, 2048], P(('grp', 'chol')), parts along dimension 0, may hold values from -6 to 6
Outputs:
- shifted_field: float32 [512, 2048], P(('grp', 'chol')), parts along dimension 0
The draws below stay inside these ranges and needn't reach their ends.
There are 2 independent parts, one for each index of `grp`. The reference program is written for one: setup_inputs(seed, part) draws one part's arguments, and reference() takes and returns one part's arrays. A program takes and returns all parts, laid end to end along the dimension named above; an argument that names none is the same for every part. Nothing has to cross between parts.
Inputs may be any that keep to these rules, and one draw needn't show every extreme that they name: `walker_order`: each row of greens appears once.
All inputs are finite; a program needn't handle non-finite values.
Results may differ from the reference program's by a relative error of at most 0.0012.
Values may be sent and summed in bfloat16 or wider, within the bound.
No kernel may reach another device: no remote copies, remote signals or barrier semaphores. Data moves between devices by JAX's collectives and lax.ppermute only.
A program may use at most 64 MiB of HBM per device.

```python
import jax
import jax.numpy as jnp

NCHOL = 2048
NP = 32768
W = 256


def strengthened(result, stream_key, source, target, shards_of, factor):
    def block_of(axis_at):
        return (jnp.arange(result.shape[axis_at]) // (result.shape[axis_at] // shards_of)).reshape((-1,) + (1,) * (result.ndim - 1 - axis_at))

    one_side = jax.random.permutation(stream_key, shards_of)[block_of(target)]
    other_side = (block_of(target) + shards_of // 2) % shards_of
    return jnp.where((block_of(source) == one_side) | (block_of(source) == other_side), factor * result, result)


def shard_levels(stream_key, dims, cuts, low, high):
    loudness = 1.0
    for dim, shards_of in cuts:
        draws = jax.random.uniform(jax.random.fold_in(jax.random.fold_in(stream_key, 6), dim), (shards_of,), jnp.float32, low / len(cuts), high / len(cuts))
        loudness = loudness * jnp.repeat(jnp.exp(draws), dims[dim] // shards_of).reshape((-1,) + (1,) * (len(dims) - 1 - dim))
    return loudness


def normal_values(key, shape, deviation, most, pieces=(), dtype=jnp.bfloat16):
    result = jax.random.normal(key, shape, jnp.float32) * deviation
    if len(pieces) > 0:
        result = shard_levels(key, shape, pieces, -0.22, 0.18) * result
    return jnp.clip(result, min=-most, max=most).astype(dtype)


def gaussian_with(own_key, shape, deviation, most, pieces, heavy, held_as=jnp.bfloat16):
    drawn = deviation * jax.random.normal(own_key, shape, jnp.float32)
    if pieces:
        drawn = drawn * shard_levels(own_key, shape, pieces, -0.22, 0.18)
    return jnp.clip(strengthened(drawn, jax.random.fold_in(own_key, 3), *heavy), -most, most).astype(held_as)


def setup_inputs(seed: int = 0, part: int = 0) -> dict:
    seeds = jax.random.split(jax.random.key(seed), 6)
    own_keys = jax.random.split(jax.random.fold_in(seeds[5], part), 6)
    chol_vectors = normal_values(seeds[0], (NCHOL, NP), NP ** -0.5, 0.03125, ((1, 16),))
    mean_greens = normal_values(seeds[1], (NP,), 1.0, 6.0, ((0, 16),))
    greens = gaussian_with(own_keys[2], (W, NP), 1.0, 6.0, ((0, 16),), (1, 0, 16, 2.0))
    walker_order = jax.random.permutation(own_keys[3], W).astype(jnp.int32)
    noise_field = normal_values(own_keys[4], (W, NCHOL), 1.0, 6.0, ((0, 16),), jnp.float32)
    return {"chol_vectors": chol_vectors, "mean_greens": mean_greens, "greens": greens, "walker_order": walker_order, "noise_field": noise_field}


def reference(chol_vectors, mean_greens, greens, walker_order, noise_field):
    picked = jnp.take(greens, walker_order.astype(jnp.int32), axis=0)
    raw_bias = jnp.dot(picked, chol_vectors.T, preferred_element_type=jnp.float32)
    mean_field = jnp.dot(chol_vectors, mean_greens, preferred_element_type=jnp.float32)
    shift = jnp.tanh(raw_bias) - mean_field[None, :]
    return noise_field - shift
```

```python
import functools

import jax
import jax.numpy as jnp
from jax import lax
from jax.experimental import pallas as pl
from jax.experimental.pallas import tpu as pltpu
from jax.sharding import PartitionSpec as P

F32, BF16 = jnp.float32, jnp.bfloat16
VMEM_BYTES = 56 * 2**20


def stage_radices(chips):
    radices = []
    while chips > 1:
        radix = 4 if chips % 4 == 0 else 2
        radices.append(radix)
        chips //= radix
    return radices


def swap(x, mask, n):
    return lax.ppermute(x, "chol", [(i, i ^ mask) for i in range(n)])


def bias_kernel(index_ref, rows_ref, chol_ref, keep_ref, send_ref, picked):
    half = keep_ref.shape[0]

    @pl.when(pl.program_id(0) == 0)
    def _():
        walkers = rows_ref.shape[0]
        chosen = index_ref[...] == lax.broadcasted_iota(jnp.int32, (2 * half, walkers), 1)
        picked[...] = jnp.dot(
            chosen.astype(BF16), rows_ref[...], preferred_element_type=F32
        ).astype(BF16)

    part = lax.dot_general(
        picked[...], chol_ref[...], (((1,), (1,)), ((), ())), preferred_element_type=F32
    )
    keep_ref[...] = part[:half]
    send_ref[...] = part[half:].astype(BF16)


def partial_bias(index, rows, chol, tile):
    slots, (nchol, pairs) = index.shape[0], chol.shape
    half = slots // 2
    return pl.pallas_call(
        bias_kernel,
        grid=(nchol // tile,),
        in_specs=[
            pl.BlockSpec((slots, 1), lambda g: (0, 0)),
            pl.BlockSpec(rows.shape, lambda g: (0, 0)),
            pl.BlockSpec((tile, pairs), lambda g: (g, 0)),
        ],
        out_specs=[pl.BlockSpec((half, tile), lambda g: (0, g))] * 2,
        out_shape=[
            jax.ShapeDtypeStruct((half, nchol), F32),
            jax.ShapeDtypeStruct((half, nchol), BF16),
        ],
        scratch_shapes=[pltpu.VMEM((slots, pairs), BF16)],
        compiler_params=pltpu.CompilerParams(vmem_limit_bytes=VMEM_BYTES),
        cost_estimate=pl.CostEstimate(
            flops=2 * slots * pairs * (nchol + rows.shape[0]),
            bytes_accessed=2 * nchol * pairs + 2 * rows.size + 6 * half * nchol,
            transcendentals=0,
        ),
    )(index, rows, chol)


def reduce_over_chips(held, radices, bit, n):
    if not radices:
        return held
    radix, rest = radices[0], radices[1:]
    later = 1
    for r in rest:
        later *= r
    rows, g = held.shape[-2:]
    held = held.reshape(radix, later, rows, g)
    shift = radix.bit_length() - 1
    total = held[0]
    if later > 1:
        onward = total[1:] + sum(
            swap(held[m, 1:].astype(BF16), m << bit, n).astype(F32) for m in range(1, radix)
        )
    mine = total[0] + sum(
        swap(held[m, 0].astype(BF16), m << bit, n).astype(F32) for m in range(1, radix)
    )
    if later == 1:
        return mine
    return reduce_over_chips(
        jnp.concatenate([mine[None], onward], axis=0), rest, bit + shift, n
    )


def per_device(n, chol_vectors, mean_greens, greens, walker_order, noise_field):
    me = lax.axis_index("chol")
    own = greens.shape[0]
    chips = n // 2
    radices = stage_radices(chips)

    mean_field = jnp.dot(chol_vectors, mean_greens, preferred_element_type=F32)
    for bit in range(n.bit_length() - 1):
        mean_field = mean_field + swap(mean_field, 1 << bit, n)

    place = jnp.arange(n, dtype=jnp.int32)
    relative, weight, left = place // chips, 2, place % chips
    for stage, radix in enumerate(radices):
        later = 1
        for r in radices[stage + 1 :]:
            later *= r
        relative = relative + weight * (left // later)
        left, weight = left % later, weight * radix
    owners = jnp.bitwise_xor(relative, me)
    slots = (owners[:, None] * own + jnp.arange(own, dtype=jnp.int32)[None, :]).reshape(-1)
    index = walker_order[slots]

    rows = lax.all_to_all(greens, "chol", split_axis=1, concat_axis=0, tiled=True)
    keep, send = partial_bias(index[:, None], rows, chol_vectors, 512)
    held = keep + swap(send, 1, n).astype(F32)
    raw_bias = reduce_over_chips(held.reshape(chips, own, -1), radices, 1, n).reshape(own, -1)
    shift = jnp.tanh(raw_bias) - mean_field[None, :]
    return noise_field - shift


def solution(mesh):
    placed = (
        P(None, "chol"),
        P("chol"),
        P(("grp", "chol"), None),
        P("grp"),
        P(("grp", "chol"), None),
    )
    return jax.shard_map(
        functools.partial(per_device, mesh.shape["chol"]),
        mesh=mesh,
        in_specs=placed,
        out_specs=P(("grp", "chol"), None),
        check_vma=False,
    )
```

```python
import functools

import jax
import jax.numpy as jnp
from jax import lax
from jax.experimental import pallas as pl
from jax.experimental.pallas import tpu as pltpu
from jax.sharding import PartitionSpec as P

F32, F16, BF16 = jnp.float32, jnp.float16, jnp.bfloat16
DIRECT_CHIPS = 8


def stage_radices(chips):
    radices = []
    while chips > 1:
        radix = 4 if chips % 4 == 0 else 2
        radices.append(radix)
        chips //= radix
    return radices


def swap(x, mask, n):
    return lax.ppermute(x, "chol", [(i, i ^ mask) for i in range(n)])


def split_kernel(greens_ref, *refs):
    outs, sems = refs[:-1], refs[-1]
    me = lax.axis_index("chol")
    own, pairs = outs[0].shape[0] // 2, outs[0].shape[1]
    copies = []
    for m in reversed(range(len(outs))):
        for j in range(2):
            there = jnp.bitwise_xor(me, 2 * m + j)
            copy = pltpu.make_async_copy(
                greens_ref.at[:, pl.ds(pl.multiple_of(there * pairs, pairs), pairs)],
                outs[m].at[pl.ds(j * own, own)],
                sems.at[m, j],
            )
            copy.start()
            copies.append(copy)
    for copy in copies:
        copy.wait()


def split_by_chip(greens, chips):
    own, total = greens.shape
    shape = (2 * own, total // (2 * chips))
    return pl.pallas_call(
        split_kernel,
        in_specs=[pl.BlockSpec(memory_space=pl.ANY)],
        out_specs=[pl.BlockSpec(memory_space=pl.ANY)] * chips,
        out_shape=[jax.ShapeDtypeStruct(shape, greens.dtype)] * chips,
        scratch_shapes=[pltpu.SemaphoreType.DMA((chips, 2))],
        cost_estimate=pl.CostEstimate(flops=0, bytes_accessed=4 * greens.size, transcendentals=0),
    )(greens)


def collect_walkers(greens, chips, n):
    own = greens.shape[0]
    sent = split_by_chip(greens, chips)
    got = {0: sent[0]}
    for m in reversed(range(1, chips)):
        got[m] = swap(sent[m], 2 * m, n)
    near, far = range(chips // 2), range(chips // 2, chips)
    passed = [
        swap(jnp.concatenate([got[m][own:] for m in part]), 1, n) for part in (near, far)
    ]
    return jnp.concatenate([got[m][:own] for m in range(chips)] + passed)


def bias_kernel(tile, index_ref, rows_ref, chol_ref, mean_ref, noise_ref, keep_ref, send_ref, base_ref, picked):
    half, nchol = keep_ref.shape
    walkers = rows_ref.shape[0]
    chosen = index_ref[...] == lax.broadcasted_iota(jnp.int32, (2 * half, walkers), 1)
    picked[...] = jnp.dot(
        chosen.astype(BF16), rows_ref[...], preferred_element_type=F32
    ).astype(BF16)
    base_ref[...] = noise_ref[...] + mean_ref[...]

    @pl.loop(0, nchol // tile)
    def _(t):
        at = pl.ds(pl.multiple_of(t * tile, tile), tile)
        part = lax.dot_general(
            picked[...], chol_ref[at, :], (((1,), (1,)), ((), ())), preferred_element_type=F32
        )
        keep_ref[:, at] = part[:half]
        send_ref[:, at] = part[half:].astype(BF16)


def partial_bias(index, rows, chol, mean_field, noise, tile):
    slots, (nchol, pairs) = index.shape[0], chol.shape
    half = slots // 2
    return pl.pallas_call(
        functools.partial(bias_kernel, tile),
        in_specs=[pl.BlockSpec(memory_space=pltpu.VMEM)] * 5,
        out_specs=[pl.BlockSpec(memory_space=pltpu.VMEM)] * 3,
        out_shape=[
            jax.ShapeDtypeStruct((half, nchol), F32),
            jax.ShapeDtypeStruct((half, nchol), BF16),
            jax.ShapeDtypeStruct(noise.shape, F32),
        ],
        scratch_shapes=[pltpu.VMEM((slots, pairs), BF16)],
        compiler_params=pltpu.CompilerParams(vmem_limit_bytes=28 * 2**20),
        cost_estimate=pl.CostEstimate(
            flops=2 * slots * pairs * (nchol + rows.shape[0]),
            bytes_accessed=2 * nchol * pairs + 2 * rows.size + 6 * half * nchol,
            transcendentals=0,
        ),
    )(index, rows, chol, mean_field, noise)


def reduce_over_chips(held, radices, bit, n):
    if not radices:
        return held
    radix, rest = radices[0], radices[1:]
    later = 1
    for r in rest:
        later *= r
    rows, g = held.shape[-2:]
    held = held.reshape(radix, later, rows, g)
    shift = radix.bit_length() - 1
    total = held[0]
    if later > 1:
        onward = total[1:] + sum(
            swap(held[m, 1:].astype(F16), m << bit, n).astype(F32) for m in range(1, radix)
        )
    mine = total[0] + sum(
        swap(held[m, 0].astype(F16), m << bit, n).astype(F32) for m in range(1, radix)
    )
    if later == 1:
        return mine
    return reduce_over_chips(
        jnp.concatenate([mine[None], onward], axis=0), rest, bit + shift, n
    )


def per_device(n, chol_vectors, mean_greens, greens, walker_order, noise_field):
    me = lax.axis_index("chol")
    own = greens.shape[0]
    chips = n // 2
    radices = stage_radices(chips)

    mean_field = jnp.dot(chol_vectors, mean_greens, preferred_element_type=F32)
    for bit in range(n.bit_length() - 1):
        mean_field = mean_field + swap(mean_field, 1 << bit, n)

    place = jnp.arange(n, dtype=jnp.int32)
    relative, weight, left = place // chips, 2, place % chips
    for stage, radix in enumerate(radices):
        later = 1
        for r in radices[stage + 1 :]:
            later *= r
        relative = relative + weight * (left // later)
        left, weight = left % later, weight * radix
    owners = jnp.bitwise_xor(relative, me)
    index = walker_order.reshape(n, own)[owners].reshape(-1)

    if chips <= DIRECT_CHIPS:
        rows = collect_walkers(greens, chips, n)
        source = jnp.bitwise_xor(index // own, me)
        index = ((source % 2) * chips + source // 2) * own + index % own
    else:
        rows = lax.all_to_all(greens, "chol", split_axis=1, concat_axis=0, tiled=True)
    keep, send, base = partial_bias(
        index[:, None], rows, chol_vectors, mean_field[None, :], noise_field, 512
    )
    held = keep + swap(send, 1, n).astype(F32)
    raw_bias = reduce_over_chips(held.reshape(chips, own, -1), radices, 1, n).reshape(own, -1)
    return base - jnp.tanh(raw_bias)


def solution(mesh):
    placed = (
        P(None, "chol"),
        P("chol"),
        P(("grp", "chol"), None),
        P("grp"),
        P(("grp", "chol"), None),
    )
    return jax.shard_map(
        functools.partial(per_device, mesh.shape["chol"]),
        mesh=mesh,
        in_specs=placed,
        out_specs=P(("grp", "chol"), None),
        check_vma=False,
    )
```

```python
import functools

import jax
import jax.numpy as jnp
from jax import lax
from jax.experimental import pallas as pl
from jax.experimental.pallas import tpu as pltpu
from jax.sharding import PartitionSpec as P

F32, F16, BF16 = jnp.float32, jnp.float16, jnp.bfloat16
DIRECT_CHIPS = 8


def stage_radices(chips):
    radices = []
    while chips > 1:
        radix = 4 if chips % 4 == 0 else 2
        radices.append(radix)
        chips //= radix
    return radices


def swap(x, mask, n):
    return lax.ppermute(x, "chol", [(i, i ^ mask) for i in range(n)])


def split_kernel(greens_ref, *outs):
    me = lax.axis_index("chol")
    own, pairs = greens_ref.shape[0], outs[0].shape[1]
    for m, out in enumerate(outs):
        for j in range(2):
            there = pl.multiple_of(jnp.bitwise_xor(me, 2 * m + j) * pairs, pairs)
            out[pl.ds(j * own, own), :] = greens_ref[:, pl.ds(there, pairs)]


def split_by_chip(greens, chips):
    own, total = greens.shape
    shape = (2 * own, total // (2 * chips))
    return pl.pallas_call(
        split_kernel,
        in_specs=[pl.BlockSpec(memory_space=pltpu.VMEM)],
        out_specs=[pl.BlockSpec(memory_space=pltpu.VMEM)] * chips,
        out_shape=[jax.ShapeDtypeStruct(shape, greens.dtype)] * chips,
        compiler_params=pltpu.CompilerParams(vmem_limit_bytes=8 * 2**20),
        cost_estimate=pl.CostEstimate(flops=0, bytes_accessed=4 * greens.size, transcendentals=0),
    )(greens)


def after(x, *others):
    return lax.optimization_barrier((x,) + others)[0]


def collect_walkers(greens, chips, n):
    own = greens.shape[0]
    sent = split_by_chip(greens, chips)
    got = [sent[0]]
    free = 2
    for m in range(1, chips):
        ended = m - chips // 2 - free + 1
        message = sent[m] if ended < 1 else after(sent[m], got[ended])
        got.append(swap(message, 2 * m, n))
    near, far = got[: chips // 2], got[chips // 2 :]
    passed = [swap(jnp.concatenate([x[own:] for x in part]), 1, n) for part in (near, far)]
    return jnp.concatenate([x[:own] for x in got] + passed), near[-1]


def mean_kernel(parts, chol_ref, mean_ref, part_ref, staged_ref, sems):
    step = chol_ref.shape[0] // parts
    copies = []
    for t in range(parts):
        at = pl.ds(t * step, step)
        copies.append(pltpu.make_async_copy(chol_ref.at[at], staged_ref.at[at], sems.at[t]))
        copies[-1].start()
    mean = jnp.broadcast_to(mean_ref[...], (8, mean_ref.shape[1]))
    for t, copy in enumerate(copies):
        copy.wait()
        at = pl.ds(t * step, step)
        part = lax.dot_general(
            mean, staged_ref[at, :], (((1,), (1,)), ((), ())), preferred_element_type=F32
        )
        part_ref[:, at] = part[:1]


def mean_part(chol, mean, parts=8):
    return pl.pallas_call(
        functools.partial(mean_kernel, parts),
        in_specs=[pl.BlockSpec(memory_space=pl.ANY), pl.BlockSpec(memory_space=pltpu.VMEM)],
        out_specs=[pl.BlockSpec(memory_space=pltpu.VMEM)] * 2,
        out_shape=[
            jax.ShapeDtypeStruct((1, chol.shape[0]), F32),
            jax.ShapeDtypeStruct(chol.shape, chol.dtype),
        ],
        scratch_shapes=[pltpu.SemaphoreType.DMA((parts,))],
        compiler_params=pltpu.CompilerParams(vmem_limit_bytes=20 * 2**20),
        cost_estimate=pl.CostEstimate(
            flops=16 * chol.size, bytes_accessed=2 * chol.size, transcendentals=0
        ),
    )(chol, mean)


def bias_kernel(tile, index_ref, rows_ref, chol_ref, keep_ref, send_ref, picked):
    half, nchol = keep_ref.shape
    walkers = rows_ref.shape[0]
    chosen = index_ref[...] == lax.broadcasted_iota(jnp.int32, (2 * half, walkers), 1)
    picked[...] = jnp.dot(
        chosen.astype(BF16), rows_ref[...], preferred_element_type=F32
    ).astype(BF16)

    @pl.loop(0, nchol // tile)
    def _(t):
        at = pl.ds(pl.multiple_of(t * tile, tile), tile)
        part = lax.dot_general(
            picked[...], chol_ref[at, :], (((1,), (1,)), ((), ())), preferred_element_type=F32
        )
        keep_ref[:, at] = part[:half]
        send_ref[:, at] = part[half:].astype(BF16)


def partial_bias(index, rows, chol, tile):
    slots, (nchol, pairs) = index.shape[0], chol.shape
    half = slots // 2
    return pl.pallas_call(
        functools.partial(bias_kernel, tile),
        in_specs=[pl.BlockSpec(memory_space=pltpu.VMEM)] * 3,
        out_specs=[pl.BlockSpec(memory_space=pltpu.VMEM)] * 2,
        out_shape=[
            jax.ShapeDtypeStruct((half, nchol), F32),
            jax.ShapeDtypeStruct((half, nchol), BF16),
        ],
        scratch_shapes=[pltpu.VMEM((slots, pairs), BF16)],
        compiler_params=pltpu.CompilerParams(vmem_limit_bytes=28 * 2**20),
        cost_estimate=pl.CostEstimate(
            flops=2 * slots * pairs * (nchol + rows.shape[0]),
            bytes_accessed=2 * nchol * pairs + 2 * rows.size + 6 * half * nchol,
            transcendentals=0,
        ),
    )(index, rows, chol)


def swap_both(x, extra, mask, n):
    got = swap(jnp.concatenate([x, extra], axis=-1).astype(F16), mask, n).astype(F32)
    return got[..., : x.shape[-1]], got[..., x.shape[-1] :]


def reduce_over_chips(held, mean, radices, bit, n):
    radix, rest = radices[0], radices[1:]
    later = held.shape[0] // radix
    held = held.reshape((radix, later) + held.shape[1:])
    masks = [m << bit for m in range(radix)]
    mine, near = held[0, 0], [held[m, 0] for m in range(1, radix)]
    if later == 1:
        for m in range(1, radix):
            got, got_mean = swap_both(near[m - 1], mean, masks[m], n)
            mine, mean = mine + got, mean + got_mean
        return mine, mean
    onward, more = held[0, 1:], mean
    for m in range(1, radix):
        if later == 2:
            got, got_mean = swap_both(held[m, 1], mean, masks[m], n)
            got = got[None]
        else:
            got = swap(held[m, 1:].astype(F16), masks[m], n).astype(F32)
            got_mean = swap(mean, masks[m], n)
        onward, more = onward + got, more + got_mean
    near, onward = lax.optimization_barrier(([x.astype(F16) for x in near], onward))
    for m in range(1, radix):
        mine = mine + swap(near[m - 1], masks[m], n).astype(F32)
    return reduce_over_chips(
        jnp.concatenate([mine[None], onward]), more, rest, bit + radix.bit_length() - 1, n
    )


def per_device(n, chol_vectors, mean_greens, greens, walker_order, noise_field):
    me = lax.axis_index("chol")
    own = greens.shape[0]
    chips = n // 2
    radices = stage_radices(chips)

    place = jnp.arange(n, dtype=jnp.int32)
    relative, weight, left = place // chips, 2, place % chips
    for stage, radix in enumerate(radices):
        later = 1
        for r in radices[stage + 1 :]:
            later *= r
        relative = relative + weight * (left // later)
        left, weight = left % later, weight * radix
    owners = jnp.bitwise_xor(relative, me)
    index = walker_order.reshape(n, own)[owners].reshape(-1)

    if chips <= DIRECT_CHIPS:
        rows, ended = collect_walkers(greens, chips, n)
        mean_greens = after(mean_greens, ended)
        source = jnp.bitwise_xor(index // own, me)
        index = ((source % 2) * chips + source // 2) * own + index % own
    else:
        rows = lax.all_to_all(greens, "chol", split_axis=1, concat_axis=0, tiled=True)
    mean, chol = mean_part(chol_vectors, mean_greens[None, :])
    mean = mean.reshape(own, -1)
    mean = mean + swap(mean, 1, n)
    keep, send = partial_bias(index[:, None], after(rows, mean), chol, 512)
    held = keep + swap(send, 1, n).astype(F32)
    raw_bias, mean = reduce_over_chips(held.reshape(chips, own, -1), mean, radices, 1, n)
    return noise_field - (jnp.tanh(raw_bias) - mean.reshape(1, -1))


def solution(mesh):
    placed = (
        P(None, "chol"),
        P("chol"),
        P(("grp", "chol"), None),
        P("grp"),
        P(("grp", "chol"), None),
    )
    return jax.shard_map(
        functools.partial(per_device, mesh.shape["chol"]),
        mesh=mesh,
        in_specs=placed,
        out_specs=P(("grp", "chol"), None),
        check_vma=False,
    )
```

```python
import functools

import jax
import jax.numpy as jnp
from jax import lax
from jax.experimental import pallas as pl
from jax.experimental.pallas import tpu as pltpu
from jax.sharding import PartitionSpec as P

F32, F16, BF16 = jnp.float32, jnp.float16, jnp.bfloat16
DIRECT_CHIPS = 8


def stage_radices(chips):
    radices = []
    while chips > 1:
        radix = 4 if chips % 4 == 0 else 2
        radices.append(radix)
        chips //= radix
    return radices


def swap(x, mask, n):
    return lax.ppermute(x, "chol", [(i, i ^ mask) for i in range(n)])


def split_kernel(greens_ref, *outs):
    me = lax.axis_index("chol")
    own, pairs = greens_ref.shape[0], outs[0].shape[1]
    for m, out in enumerate(outs):
        for j in range(2):
            there = pl.multiple_of(jnp.bitwise_xor(me, 2 * m + j) * pairs, pairs)
            out[pl.ds(j * own, own), :] = greens_ref[:, pl.ds(there, pairs)]


def split_by_chip(greens, chips):
    own, total = greens.shape
    shape = (2 * own, total // (2 * chips))
    return pl.pallas_call(
        split_kernel,
        in_specs=[pl.BlockSpec(memory_space=pltpu.VMEM)],
        out_specs=[pl.BlockSpec(memory_space=pltpu.VMEM)] * chips,
        out_shape=[jax.ShapeDtypeStruct(shape, greens.dtype)] * chips,
        compiler_params=pltpu.CompilerParams(vmem_limit_bytes=8 * 2**20),
        cost_estimate=pl.CostEstimate(flops=0, bytes_accessed=4 * greens.size, transcendentals=0),
    )(greens)


def after(x, *others):
    return lax.optimization_barrier((x,) + others)[0]


def collect_walkers(greens, chips, n):
    own = greens.shape[0]
    sent = split_by_chip(greens, chips)
    waits = {3: 1, 5: 2, 7: 3} if chips == 8 else {}
    got = [sent[0]]
    for m in range(1, chips):
        message = after(sent[m], got[waits[m]]) if m in waits else sent[m]
        got.append(swap(message, 2 * m, n))
    near, far = got[: chips // 2], got[chips // 2 :]
    passed = [swap(jnp.concatenate([x[own:] for x in part]), 1, n) for part in (near, far)]
    return jnp.concatenate([x[:own] for x in got] + passed), got[chips // 4]


def mean_kernel(parts, chol_ref, mean_ref, part_ref, staged_ref, sems):
    step = chol_ref.shape[0] // parts
    copies = []
    for t in range(parts):
        at = pl.ds(t * step, step)
        copies.append(pltpu.make_async_copy(chol_ref.at[at], staged_ref.at[at], sems.at[t]))
        copies[-1].start()
    mean = jnp.broadcast_to(mean_ref[...], (8, mean_ref.shape[1]))
    for t, copy in enumerate(copies):
        copy.wait()
        at = pl.ds(t * step, step)
        part = lax.dot_general(
            mean, staged_ref[at, :], (((1,), (1,)), ((), ())), preferred_element_type=F32
        )
        part_ref[:, at] = part[:1]


def mean_part(chol, mean, parts=8):
    return pl.pallas_call(
        functools.partial(mean_kernel, parts),
        in_specs=[pl.BlockSpec(memory_space=pl.ANY), pl.BlockSpec(memory_space=pltpu.VMEM)],
        out_specs=[pl.BlockSpec(memory_space=pltpu.VMEM)] * 2,
        out_shape=[
            jax.ShapeDtypeStruct((1, chol.shape[0]), F32),
            jax.ShapeDtypeStruct(chol.shape, chol.dtype),
        ],
        scratch_shapes=[pltpu.SemaphoreType.DMA((parts,))],
        compiler_params=pltpu.CompilerParams(vmem_limit_bytes=40 * 2**20),
        cost_estimate=pl.CostEstimate(
            flops=16 * chol.size, bytes_accessed=2 * chol.size, transcendentals=0
        ),
    )(chol, mean)


def bias_kernel(tile, index_ref, rows_ref, chol_ref, keep_ref, send_ref, picked):
    half, nchol = keep_ref.shape
    walkers = rows_ref.shape[0]
    chosen = index_ref[...] == lax.broadcasted_iota(jnp.int32, (2 * half, walkers), 1)
    picked[...] = jnp.dot(
        chosen.astype(BF16), rows_ref[...], preferred_element_type=F32
    ).astype(BF16)

    @pl.loop(0, nchol // tile)
    def _(t):
        at = pl.ds(pl.multiple_of(t * tile, tile), tile)
        part = lax.dot_general(
            picked[...], chol_ref[at, :], (((1,), (1,)), ((), ())), preferred_element_type=F32
        )
        keep_ref[:, at] = part[:half]
        send_ref[:, at] = part[half:].astype(BF16)


def partial_bias(index, rows, chol, tile):
    slots, (nchol, pairs) = index.shape[0], chol.shape
    half = slots // 2
    return pl.pallas_call(
        functools.partial(bias_kernel, tile),
        in_specs=[pl.BlockSpec(memory_space=pltpu.VMEM)] * 3,
        out_specs=[pl.BlockSpec(memory_space=pltpu.VMEM)] * 2,
        out_shape=[
            jax.ShapeDtypeStruct((half, nchol), F32),
            jax.ShapeDtypeStruct((half, nchol), BF16),
        ],
        scratch_shapes=[pltpu.VMEM((slots, pairs), BF16)],
        compiler_params=pltpu.CompilerParams(vmem_limit_bytes=28 * 2**20),
        cost_estimate=pl.CostEstimate(
            flops=2 * slots * pairs * (nchol + rows.shape[0]),
            bytes_accessed=2 * nchol * pairs + 2 * rows.size + 6 * half * nchol,
            transcendentals=0,
        ),
    )(index, rows, chol)


def swap_both(x, extra, mask, n):
    blocks, rows, g = x.shape
    extra = jnp.pad(extra[None], ((0, blocks - 1), (0, 0), (0, 0)))
    sent = jnp.concatenate([x, extra], axis=-1).astype(F16).reshape(blocks * rows, -1)
    got = swap(sent, mask, n).astype(F32).reshape(blocks, rows, -1)
    return got[..., :g], got[0, :, g:]


def reduce_over_chips(held, mean, radices, n):
    bit, mine = 1, []
    for i, radix in enumerate(radices):
        held = held.reshape((radix, held.shape[0] // radix) + held.shape[1:])
        total, mean_total = held[0], mean
        split = radix == 4 and i < len(radices) - 1
        for m in (3, 1, 2) if radix == 4 else (1,):
            skip = 1 if split and m == 3 else 0
            got, got_mean = swap_both(held[m, skip:], mean, m << bit, n)
            got = jnp.pad(got, ((skip, 0), (0, 0), (0, 0)))
            total, mean_total = total + got, mean_total + got_mean
        if split:
            mine.append(swap(held[3, 0].astype(F16), 3 << bit, n).astype(F32))
        held, mean = total, mean_total
        bit += radix.bit_length() - 1
    return held[0] + sum(mine), mean


def per_device(n, chol_vectors, mean_greens, greens, walker_order, noise_field):
    me = lax.axis_index("chol")
    own = greens.shape[0]
    chips = n // 2
    radices = stage_radices(chips)

    place = jnp.arange(n, dtype=jnp.int32)
    relative, weight, left = place // chips, 2, place % chips
    for stage, radix in enumerate(radices):
        later = 1
        for r in radices[stage + 1 :]:
            later *= r
        relative = relative + weight * (left // later)
        left, weight = left % later, weight * radix
    owners = jnp.bitwise_xor(relative, me)
    index = walker_order.reshape(n, own)[owners].reshape(-1)

    if chips <= DIRECT_CHIPS:
        rows, ended = collect_walkers(greens, chips, n)
        mean_greens = after(mean_greens, ended)
        source = jnp.bitwise_xor(index // own, me)
        index = ((source % 2) * chips + source // 2) * own + index % own
    else:
        rows = lax.all_to_all(greens, "chol", split_axis=1, concat_axis=0, tiled=True)
    mean, chol = mean_part(chol_vectors, mean_greens[None, :])
    mean = mean.reshape(own, -1)
    mean = mean + swap(mean, 1, n)
    keep, send = partial_bias(index[:, None], after(rows, mean), chol, 512)
    held = keep + swap(send, 1, n).astype(F32)
    raw_bias, mean = reduce_over_chips(held.reshape(chips, own, -1), mean, radices, n)
    return noise_field - (jnp.tanh(raw_bias) - mean.reshape(1, -1))


def solution(mesh):
    placed = (
        P(None, "chol"),
        P("chol"),
        P(("grp", "chol"), None),
        P("grp"),
        P(("grp", "chol"), None),
    )
    return jax.shard_map(
        functools.partial(per_device, mesh.shape["chol"]),
        mesh=mesh,
        in_specs=placed,
        out_specs=P(("grp", "chol"), None),
        check_vma=False,
    )
```

```python
import functools

import jax
import jax.numpy as jnp
from jax import lax
from jax.experimental import pallas as pl
from jax.experimental.pallas import tpu as pltpu
from jax.sharding import PartitionSpec as P

F32, F16, BF16 = jnp.float32, jnp.float16, jnp.bfloat16
DIRECT_CHIPS = 8


def stage_radices(chips):
    radices = []
    while chips > 1:
        radix = 4 if chips % 4 == 0 else 2
        radices.append(radix)
        chips //= radix
    return radices


def swap(x, mask, n):
    return lax.ppermute(x, "chol", [(i, i ^ mask) for i in range(n)])


def split_kernel(greens_ref, *outs):
    me = lax.axis_index("chol")
    own = greens_ref.shape[0]
    pairs = outs[0].shape[1]
    far = len(outs) - 2
    for m in range(2 * far):
        for j in range(2):
            there = pl.multiple_of(jnp.bitwise_xor(me, 2 * m + j) * pairs, pairs)
            out, at = (outs[j], m) if m < far else (outs[2 + m - far], j)
            out[pl.ds(at * own, own), :] = greens_ref[:, pl.ds(there, pairs)]


def split_by_device(greens, n):
    own, total = greens.shape
    pairs = total // n
    shapes = [(n // 4 * own, pairs)] * 2 + [(2 * own, pairs)] * (n // 4)
    outs = pl.pallas_call(
        split_kernel,
        in_specs=[pl.BlockSpec(memory_space=pltpu.VMEM)],
        out_specs=[pl.BlockSpec(memory_space=pltpu.VMEM)] * len(shapes),
        out_shape=[jax.ShapeDtypeStruct(shape, greens.dtype) for shape in shapes],
        compiler_params=pltpu.CompilerParams(vmem_limit_bytes=8 * 2**20),
        cost_estimate=pl.CostEstimate(flops=0, bytes_accessed=4 * greens.size, transcendentals=0),
    )(greens)
    return outs[0], outs[1], outs[2:]


def after(x, *others):
    return lax.optimization_barrier((x,) + others)[0]


def collect_walkers(greens, n):
    own, half = greens.shape[0], n // 4
    near, other, far = split_by_device(greens, n)
    other = swap(other, 1, n)
    block = lambda x, i: x[i * own : (i + 1) * own]
    sent = [jnp.concatenate([block(near, i), block(other, i)]) for i in range(half)] + list(far)
    waits = {5: 1, 7: 2} if half == 4 else {}
    got = [sent[0]]
    for m in range(1, 2 * half):
        message = after(sent[m], got[waits[m]]) if m in waits else sent[m]
        got.append(swap(message, 2 * m, n))
    passed = swap(jnp.concatenate([x[own:] for x in got[half:]]), 1, n)
    return jnp.concatenate(got[:half] + [x[:own] for x in got[half:]] + [passed]), got[1]


def place_of_source(source, n):
    far = n // 2 + (source % 2) * (n // 4) + (source - n // 2) // 2
    return jnp.where(source < n // 2, source, far)


def mean_kernel(parts, chol_ref, mean_ref, part_ref, staged_ref, sems):
    step = chol_ref.shape[0] // parts
    copies = []
    for t in range(parts):
        at = pl.ds(t * step, step)
        copies.append(pltpu.make_async_copy(chol_ref.at[at], staged_ref.at[at], sems.at[t]))
    for copy in copies[:2]:
        copy.start()
    mean = jnp.broadcast_to(mean_ref[...], (8, mean_ref.shape[1]))
    for t, copy in enumerate(copies):
        copy.wait()
        if t + 2 < parts:
            copies[t + 2].start()
        at = pl.ds(t * step, step)
        part = lax.dot_general(
            mean, staged_ref[at, :], (((1,), (1,)), ((), ())), preferred_element_type=F32
        )
        part_ref[:, at] = part[:1]


def mean_part(chol, mean, parts=4):
    return pl.pallas_call(
        functools.partial(mean_kernel, parts),
        in_specs=[pl.BlockSpec(memory_space=pl.ANY), pl.BlockSpec(memory_space=pltpu.VMEM)],
        out_specs=[pl.BlockSpec(memory_space=pltpu.VMEM)] * 2,
        out_shape=[
            jax.ShapeDtypeStruct((1, chol.shape[0]), F32),
            jax.ShapeDtypeStruct(chol.shape, chol.dtype),
        ],
        scratch_shapes=[pltpu.SemaphoreType.DMA((parts,))],
        compiler_params=pltpu.CompilerParams(vmem_limit_bytes=40 * 2**20),
        cost_estimate=pl.CostEstimate(
            flops=16 * chol.size, bytes_accessed=2 * chol.size, transcendentals=0
        ),
    )(chol, mean)


def bias_kernel(tile, index_ref, rows_ref, chol_ref, keep_ref, send_ref, picked):
    half, nchol = keep_ref.shape
    walkers = rows_ref.shape[0]
    chosen = index_ref[...] == lax.broadcasted_iota(jnp.int32, (2 * half, walkers), 1)
    picked[...] = jnp.dot(
        chosen.astype(BF16), rows_ref[...], preferred_element_type=F32
    ).astype(BF16)

    @pl.loop(0, nchol // tile)
    def _(t):
        at = pl.ds(pl.multiple_of(t * tile, tile), tile)
        part = lax.dot_general(
            picked[...], chol_ref[at, :], (((1,), (1,)), ((), ())), preferred_element_type=F32
        )
        keep_ref[:, at] = part[:half]
        send_ref[:, at] = part[half:].astype(BF16)


def partial_bias(index, rows, chol, tile):
    slots, (nchol, pairs) = index.shape[0], chol.shape
    half = slots // 2
    return pl.pallas_call(
        functools.partial(bias_kernel, tile),
        in_specs=[pl.BlockSpec(memory_space=pltpu.VMEM)] * 3,
        out_specs=[pl.BlockSpec(memory_space=pltpu.VMEM)] * 2,
        out_shape=[
            jax.ShapeDtypeStruct((half, nchol), F32),
            jax.ShapeDtypeStruct((half, nchol), BF16),
        ],
        scratch_shapes=[pltpu.VMEM((slots, pairs), BF16)],
        compiler_params=pltpu.CompilerParams(vmem_limit_bytes=28 * 2**20),
        cost_estimate=pl.CostEstimate(
            flops=2 * slots * pairs * (nchol + rows.shape[0]),
            bytes_accessed=2 * nchol * pairs + 2 * rows.size + 6 * half * nchol,
            transcendentals=0,
        ),
    )(index, rows, chol)


def swap_both(x, extra, mask, n):
    blocks, rows, g = x.shape
    extra = jnp.pad(extra[None], ((0, blocks - 1), (0, 0), (0, 0)))
    sent = jnp.concatenate([x, extra], axis=-1).astype(F16).reshape(blocks * rows, -1)
    got = swap(sent, mask, n).astype(F32).reshape(blocks, rows, -1)
    return got[..., :g], got[0, :, g:]


def reduce_over_chips(held, mean, radices, n):
    bit, mine = 1, []
    for i, radix in enumerate(radices):
        held = held.reshape((radix, held.shape[0] // radix) + held.shape[1:])
        total, mean_total = held[0], mean
        split = radix == 4 and i < len(radices) - 1
        for m in (3, 1, 2) if radix == 4 else (1,):
            skip = 1 if split and m == 3 else 0
            got, got_mean = swap_both(held[m, skip:], mean, m << bit, n)
            got = jnp.pad(got, ((skip, 0), (0, 0), (0, 0)))
            total, mean_total = total + got, mean_total + got_mean
        if split:
            mine.append(swap(held[3, 0].astype(F16), 3 << bit, n).astype(F32))
        held, mean = total, mean_total
        bit += radix.bit_length() - 1
    return held[0] + sum(mine), mean


def per_device(n, chol_vectors, mean_greens, greens, walker_order, noise_field):
    me = lax.axis_index("chol")
    own = greens.shape[0]
    chips = n // 2
    radices = stage_radices(chips)

    place = jnp.arange(n, dtype=jnp.int32)
    relative, weight, left = place // chips, 2, place % chips
    for stage, radix in enumerate(radices):
        later = 1
        for r in radices[stage + 1 :]:
            later *= r
        relative = relative + weight * (left // later)
        left, weight = left % later, weight * radix
    owners = jnp.bitwise_xor(relative, me)
    index = walker_order.reshape(n, own)[owners].reshape(-1)

    mean_row = mean_greens[None, :]
    if chips <= DIRECT_CHIPS:
        rows, ended = collect_walkers(greens, n)
        mean_row = after(mean_row, ended)
        source = jnp.bitwise_xor(index // own, me)
        index = place_of_source(source, n) * own + index % own
    else:
        rows = lax.all_to_all(greens, "chol", split_axis=1, concat_axis=0, tiled=True)
    mean, chol = mean_part(chol_vectors, mean_row)
    mean = mean.reshape(own, -1)
    mean = mean + swap(mean, 1, n)
    keep, send = partial_bias(index[:, None], after(rows, mean), chol, 512)
    held = keep + swap(send, 1, n).astype(F32)
    raw_bias, mean = reduce_over_chips(held.reshape(chips, own, -1), mean, radices, n)
    return noise_field - (jnp.tanh(raw_bias) - mean.reshape(1, -1))


def solution(mesh):
    placed = (
        P(None, "chol"),
        P("chol"),
        P(("grp", "chol"), None),
        P("grp"),
        P(("grp", "chol"), None),
    )
    return jax.shard_map(
        functools.partial(per_device, mesh.shape["chol"]),
        mesh=mesh,
        in_specs=placed,
        out_specs=P(("grp", "chol"), None),
        check_vma=False,
    )
```

```python
import functools

import jax
import jax.numpy as jnp
from jax import lax
from jax.experimental import pallas as pl
from jax.experimental.pallas import tpu as pltpu
from jax.sharding import PartitionSpec as P

F32, F16, BF16 = jnp.float32, jnp.float16, jnp.bfloat16
DIRECT_CHIPS = 8


def stage_radices(chips):
    radices = []
    while chips > 1:
        radix = 4 if chips % 4 == 0 else 2
        radices.append(radix)
        chips //= radix
    return radices


def swap(x, mask, n):
    return lax.ppermute(x, "chol", [(i, i ^ mask) for i in range(n)])


def split_kernel(greens_ref, *outs):
    me = lax.axis_index("chol")
    own = greens_ref.shape[0]
    pairs = outs[0].shape[1]
    far = len(outs) - 2
    for m in range(2 * far):
        for j in range(2):
            there = pl.multiple_of(jnp.bitwise_xor(me, 2 * m + j) * pairs, pairs)
            out, at = (outs[j], m) if m < far else (outs[2 + m - far], j)
            out[pl.ds(at * own, own), :] = greens_ref[:, pl.ds(there, pairs)]


def split_by_device(greens, n):
    own, total = greens.shape
    pairs = total // n
    shapes = [(n // 4 * own, pairs)] * 2 + [(2 * own, pairs)] * (n // 4)
    outs = pl.pallas_call(
        split_kernel,
        in_specs=[pl.BlockSpec(memory_space=pltpu.VMEM)],
        out_specs=[pl.BlockSpec(memory_space=pltpu.VMEM)] * len(shapes),
        out_shape=[jax.ShapeDtypeStruct(shape, greens.dtype) for shape in shapes],
        compiler_params=pltpu.CompilerParams(vmem_limit_bytes=8 * 2**20),
        cost_estimate=pl.CostEstimate(flops=0, bytes_accessed=4 * greens.size, transcendentals=0),
    )(greens)
    return outs[0], outs[1], outs[2:]


def after(x, *others):
    return lax.optimization_barrier((x,) + others)[0]


def collect_walkers(greens, n):
    own, half = greens.shape[0], n // 4
    near, other, far = split_by_device(greens, n)
    other = swap(other, 1, n)
    block = lambda x, i: x[i * own : (i + 1) * own]
    sent = [jnp.concatenate([block(near, i), block(other, i)]) for i in range(half)] + list(far)
    waits = {5: 1, 7: 2} if half == 4 else {}
    got = [sent[0]]
    for m in range(1, 2 * half):
        message = after(sent[m], got[waits[m]]) if m in waits else sent[m]
        got.append(swap(message, 2 * m, n))
    passed = [swap(jnp.concatenate([x[own:] for x in part]), 1, n) for part in (got[half:-1], got[-1:])]
    return jnp.concatenate(got[:half] + [x[:own] for x in got[half:]] + passed), got[1]


def place_of_source(source, n):
    far = n // 2 + (source % 2) * (n // 4) + (source - n // 2) // 2
    return jnp.where(source < n // 2, source, far)


def mean_kernel(parts, chol_ref, mean_ref, part_ref, staged_ref, sems):
    step = chol_ref.shape[0] // parts
    copies = []
    for t in range(parts):
        at = pl.ds(t * step, step)
        copies.append(pltpu.make_async_copy(chol_ref.at[at], staged_ref.at[at], sems.at[t]))
    for copy in copies[:2]:
        copy.start()
    mean = jnp.broadcast_to(mean_ref[...], (8, mean_ref.shape[1]))
    for t, copy in enumerate(copies):
        copy.wait()
        if t + 2 < parts:
            copies[t + 2].start()
        at = pl.ds(t * step, step)
        part = lax.dot_general(
            mean, staged_ref[at, :], (((1,), (1,)), ((), ())), preferred_element_type=F32
        )
        part_ref[:, at] = part[:1]


def mean_part(chol, mean, parts=4):
    return pl.pallas_call(
        functools.partial(mean_kernel, parts),
        in_specs=[pl.BlockSpec(memory_space=pl.ANY), pl.BlockSpec(memory_space=pltpu.VMEM)],
        out_specs=[pl.BlockSpec(memory_space=pltpu.VMEM)] * 2,
        out_shape=[
            jax.ShapeDtypeStruct((1, chol.shape[0]), F32),
            jax.ShapeDtypeStruct(chol.shape, chol.dtype),
        ],
        scratch_shapes=[pltpu.SemaphoreType.DMA((parts,))],
        compiler_params=pltpu.CompilerParams(vmem_limit_bytes=40 * 2**20),
        cost_estimate=pl.CostEstimate(
            flops=16 * chol.size, bytes_accessed=2 * chol.size, transcendentals=0
        ),
    )(chol, mean)


def bias_kernel(tile, index_ref, rows_ref, chol_ref, keep_ref, send_ref, picked):
    half, nchol = keep_ref.shape
    walkers = rows_ref.shape[0]
    chosen = index_ref[...] == lax.broadcasted_iota(jnp.int32, (2 * half, walkers), 1)
    picked[...] = jnp.dot(
        chosen.astype(BF16), rows_ref[...], preferred_element_type=F32
    ).astype(BF16)

    for t in range(nchol // tile):
        at = pl.ds(t * tile, tile)
        part = lax.dot_general(
            picked[...], chol_ref[at, :], (((1,), (1,)), ((), ())), preferred_element_type=F32
        )
        keep_ref[:, at] = part[:half]
        send_ref[:, at] = part[half:].astype(BF16)


def partial_bias(index, rows, chol, tile):
    slots, (nchol, pairs) = index.shape[0], chol.shape
    half = slots // 2
    return pl.pallas_call(
        functools.partial(bias_kernel, tile),
        in_specs=[pl.BlockSpec(memory_space=pltpu.VMEM)] * 3,
        out_specs=[pl.BlockSpec(memory_space=pltpu.VMEM)] * 2,
        out_shape=[
            jax.ShapeDtypeStruct((half, nchol), F32),
            jax.ShapeDtypeStruct((half, nchol), BF16),
        ],
        scratch_shapes=[pltpu.VMEM((slots, pairs), BF16)],
        compiler_params=pltpu.CompilerParams(vmem_limit_bytes=28 * 2**20),
        cost_estimate=pl.CostEstimate(
            flops=2 * slots * pairs * (nchol + rows.shape[0]),
            bytes_accessed=2 * nchol * pairs + 2 * rows.size + 6 * half * nchol,
            transcendentals=0,
        ),
    )(index, rows, chol)


def swap_both(x, extra, mask, n):
    blocks, rows, g = x.shape
    extra = jnp.pad(extra[None], ((0, blocks - 1), (0, 0), (0, 0)))
    sent = jnp.concatenate([x, extra], axis=-1).astype(F16).reshape(blocks * rows, -1)
    got = swap(sent, mask, n).astype(F32).reshape(blocks, rows, -1)
    return got[..., :g], got[0, :, g:]


def reduce_over_chips(held, mean, radices, n):
    bit, mine = 1, []
    for i, radix in enumerate(radices):
        held = held.reshape((radix, held.shape[0] // radix) + held.shape[1:])
        total, mean_total = held[0], mean
        split = radix == 4 and i < len(radices) - 1
        for m in (3, 1, 2) if radix == 4 else (1,):
            skip = 1 if split and m == 3 else 0
            got, got_mean = swap_both(held[m, skip:], mean, m << bit, n)
            got = jnp.pad(got, ((skip, 0), (0, 0), (0, 0)))
            total, mean_total = total + got, mean_total + got_mean
        if split:
            mine.append(swap(held[3, 0].astype(F16), 3 << bit, n).astype(F32))
        held, mean = total, mean_total
        bit += radix.bit_length() - 1
    return held[0] + sum(mine), mean


def per_device(n, chol_vectors, mean_greens, greens, walker_order, noise_field):
    me = lax.axis_index("chol")
    own = greens.shape[0]
    chips = n // 2
    radices = stage_radices(chips)

    place = jnp.arange(n, dtype=jnp.int32)
    relative, weight, left = place // chips, 2, place % chips
    for stage, radix in enumerate(radices):
        later = 1
        for r in radices[stage + 1 :]:
            later *= r
        relative = relative + weight * (left // later)
        left, weight = left % later, weight * radix
    owners = jnp.bitwise_xor(relative, me)
    index = walker_order.reshape(n, own)[owners].reshape(-1)

    mean_row = mean_greens[None, :]
    if chips <= DIRECT_CHIPS:
        rows, ended = collect_walkers(greens, n)
        mean_row = after(mean_row, ended)
        source = jnp.bitwise_xor(index // own, me)
        index = place_of_source(source, n) * own + index % own
    else:
        rows = lax.all_to_all(greens, "chol", split_axis=1, concat_axis=0, tiled=True)
    mean, chol = mean_part(chol_vectors, mean_row)
    mean = mean.reshape(own, -1)
    mean = mean + swap(mean, 1, n)
    keep, send = partial_bias(index[:, None], after(rows, mean), chol, 512)
    held = keep + swap(send, 1, n).astype(F32)
    raw_bias, mean = reduce_over_chips(held.reshape(chips, own, -1), mean, radices, n)
    return noise_field - (jnp.tanh(raw_bias) - mean.reshape(1, -1))


def solution(mesh):
    placed = (
        P(None, "chol"),
        P("chol"),
        P(("grp", "chol"), None),
        P("grp"),
        P(("grp", "chol"), None),
    )
    return jax.shard_map(
        functools.partial(per_device, mesh.shape["chol"]),
        mesh=mesh,
        in_specs=placed,
        out_specs=P(("grp", "chol"), None),
        check_vma=False,
    )
```

```python
import functools

import jax
import jax.numpy as jnp
from jax import lax
from jax.experimental import pallas as pl
from jax.experimental.pallas import tpu as pltpu
from jax.sharding import PartitionSpec as P

F32, F16, BF16 = jnp.float32, jnp.float16, jnp.bfloat16
DIRECT_CHIPS = 8


def stage_radices(chips):
    radices = []
    while chips > 1:
        radix = 4 if chips % 4 == 0 else 2
        radices.append(radix)
        chips //= radix
    return radices


def swap(x, mask, n):
    return lax.ppermute(x, "chol", [(i, i ^ mask) for i in range(n)])


def split_kernel(greens_ref, *outs):
    me = lax.axis_index("chol")
    own = greens_ref.shape[0]
    pairs = outs[0].shape[1]
    half = outs[0].shape[0] // own
    for m in range(2 * half):
        for j in range(2):
            there = pl.multiple_of(jnp.bitwise_xor(me, 2 * m + j) * pairs, pairs)
            if m < half:
                out, at = outs[j], m
            elif m < 2 * half - 1:
                out, at = outs[2 + m - half], j
            else:
                out, at = outs[1 + half + j], 0
            out[pl.ds(at * own, own), :] = greens_ref[:, pl.ds(there, pairs)]


def split_by_device(greens, n):
    own, total = greens.shape
    pairs = total // n
    half = n // 4
    rows = [half * own] * 2 + [2 * own] * (half - 1) + [own] * 2
    outs = pl.pallas_call(
        split_kernel,
        in_specs=[pl.BlockSpec(memory_space=pltpu.VMEM)],
        out_specs=[pl.BlockSpec(memory_space=pltpu.VMEM)] * len(rows),
        out_shape=[jax.ShapeDtypeStruct((r, pairs), greens.dtype) for r in rows],
        compiler_params=pltpu.CompilerParams(vmem_limit_bytes=8 * 2**20),
        cost_estimate=pl.CostEstimate(flops=0, bytes_accessed=4 * greens.size, transcendentals=0),
    )(greens)
    return outs[0], outs[1], outs[2 : half + 1], outs[half + 1 :]


def after(x, *others):
    return lax.optimization_barrier((x,) + others)[0]


def collect_walkers(greens, n):
    own, half = greens.shape[0], n // 4
    near, other, far, last = split_by_device(greens, n)
    other = swap(other, 1, n)
    block = lambda x, i: x[i * own : (i + 1) * own]
    sent = [jnp.concatenate([block(near, i), block(other, i)]) for i in range(half)] + list(far)
    waits = {5: 1} if half == 4 else {}
    got = {0: sent[0]}
    for m in range(1, 2 * half - 1):
        message = after(sent[m], got[waits[m]]) if m in waits else sent[m]
        got[m] = swap(message, 2 * m, n)
    last = [after(x, got[w]) for x, w in zip(last, (2, 3))]
    last = [swap(x, n - 2 + j, n) for j, x in enumerate(last)]
    far = [got[m] for m in range(half, 2 * half - 1)]
    passed = swap(jnp.concatenate([x[own:] for x in far]), 1, n)
    rows = [got[m] for m in range(half)] + [x[:own] for x in far] + [passed] + last
    return jnp.concatenate(rows), got[1]


def place_of_source(source, n):
    half = n // 4
    far = n // 2 + (source % 2) * (half - 1) + source // 2 - half
    return jnp.where((source < n // 2) | (source >= n - 2), source, far)


def mean_kernel(parts, chol_ref, mean_ref, part_ref, staged_ref, sems):
    step = chol_ref.shape[0] // parts
    copies = []
    for t in range(parts):
        at = pl.ds(t * step, step)
        copies.append(pltpu.make_async_copy(chol_ref.at[at], staged_ref.at[at], sems.at[t]))
    for copy in copies[:2]:
        copy.start()
    mean = jnp.broadcast_to(mean_ref[...], (8, mean_ref.shape[1]))
    for t, copy in enumerate(copies):
        copy.wait()
        if t + 2 < parts:
            copies[t + 2].start()
        at = pl.ds(t * step, step)
        part = lax.dot_general(
            mean, staged_ref[at, :], (((1,), (1,)), ((), ())), preferred_element_type=F32
        )
        part_ref[:, at] = part[:1]


def mean_part(chol, mean, parts=4):
    return pl.pallas_call(
        functools.partial(mean_kernel, parts),
        in_specs=[pl.BlockSpec(memory_space=pl.ANY), pl.BlockSpec(memory_space=pltpu.VMEM)],
        out_specs=[pl.BlockSpec(memory_space=pltpu.VMEM)] * 2,
        out_shape=[
            jax.ShapeDtypeStruct((1, chol.shape[0]), F32),
            jax.ShapeDtypeStruct(chol.shape, chol.dtype),
        ],
        scratch_shapes=[pltpu.SemaphoreType.DMA((parts,))],
        compiler_params=pltpu.CompilerParams(vmem_limit_bytes=40 * 2**20),
        cost_estimate=pl.CostEstimate(
            flops=16 * chol.size, bytes_accessed=2 * chol.size, transcendentals=0
        ),
    )(chol, mean)


def bias_kernel(tile, index_ref, rows_ref, chol_ref, keep_ref, send_ref, picked):
    half, nchol = keep_ref.shape
    walkers = rows_ref.shape[0]
    chosen = index_ref[...] == lax.broadcasted_iota(jnp.int32, (2 * half, walkers), 1)
    picked[...] = jnp.dot(
        chosen.astype(BF16), rows_ref[...], preferred_element_type=F32
    ).astype(BF16)

    for t in range(nchol // tile):
        at = pl.ds(t * tile, tile)
        part = lax.dot_general(
            picked[...], chol_ref[at, :], (((1,), (1,)), ((), ())), preferred_element_type=F32
        )
        keep_ref[:, at] = part[:half]
        send_ref[:, at] = part[half:].astype(BF16)


def partial_bias(index, rows, chol, tile):
    slots, (nchol, pairs) = index.shape[0], chol.shape
    half = slots // 2
    return pl.pallas_call(
        functools.partial(bias_kernel, tile),
        in_specs=[pl.BlockSpec(memory_space=pltpu.VMEM)] * 3,
        out_specs=[pl.BlockSpec(memory_space=pltpu.VMEM)] * 2,
        out_shape=[
            jax.ShapeDtypeStruct((half, nchol), F32),
            jax.ShapeDtypeStruct((half, nchol), BF16),
        ],
        scratch_shapes=[pltpu.VMEM((slots, pairs), BF16)],
        compiler_params=pltpu.CompilerParams(vmem_limit_bytes=28 * 2**20),
        cost_estimate=pl.CostEstimate(
            flops=2 * slots * pairs * (nchol + rows.shape[0]),
            bytes_accessed=2 * nchol * pairs + 2 * rows.size + 6 * half * nchol,
            transcendentals=0,
        ),
    )(index, rows, chol)


def swap_both(x, extra, mask, n):
    blocks, rows, g = x.shape
    extra = jnp.pad(extra[None], ((0, blocks - 1), (0, 0), (0, 0)))
    sent = jnp.concatenate([x, extra], axis=-1).astype(F16).reshape(blocks * rows, -1)
    got = swap(sent, mask, n).astype(F32).reshape(blocks, rows, -1)
    return got[..., :g], got[0, :, g:]


def reduce_over_chips(held, mean, radices, n):
    bit, mine = 1, []
    for i, radix in enumerate(radices):
        held = held.reshape((radix, held.shape[0] // radix) + held.shape[1:])
        total, mean_total = held[0], mean
        split = radix == 4 and i < len(radices) - 1
        for m in (3, 1, 2) if radix == 4 else (1,):
            skip = 1 if split and m == 3 else 0
            got, got_mean = swap_both(held[m, skip:], mean, m << bit, n)
            got = jnp.pad(got, ((skip, 0), (0, 0), (0, 0)))
            total, mean_total = total + got, mean_total + got_mean
        if split:
            mine.append(swap(held[3, 0].astype(F16), 3 << bit, n).astype(F32))
        held, mean = total, mean_total
        bit += radix.bit_length() - 1
    return held[0] + sum(mine), mean


def per_device(n, chol_vectors, mean_greens, greens, walker_order, noise_field):
    me = lax.axis_index("chol")
    own = greens.shape[0]
    chips = n // 2
    radices = stage_radices(chips)

    place = jnp.arange(n, dtype=jnp.int32)
    relative, weight, left = place // chips, 2, place % chips
    for stage, radix in enumerate(radices):
        later = 1
        for r in radices[stage + 1 :]:
            later *= r
        relative = relative + weight * (left // later)
        left, weight = left % later, weight * radix
    owners = jnp.bitwise_xor(relative, me)
    index = walker_order.reshape(n, own)[owners].reshape(-1)

    mean_row = mean_greens[None, :]
    if chips <= DIRECT_CHIPS:
        rows, ended = collect_walkers(greens, n)
        mean_row = after(mean_row, ended)
        source = jnp.bitwise_xor(index // own, me)
        index = place_of_source(source, n) * own + index % own
    else:
        rows = lax.all_to_all(greens, "chol", split_axis=1, concat_axis=0, tiled=True)
    mean, chol = mean_part(chol_vectors, mean_row)
    mean = mean.reshape(own, -1)
    mean = mean + swap(mean, 1, n)
    keep, send = partial_bias(index[:, None], after(rows, mean), chol, 512)
    held = keep + swap(send, 1, n).astype(F32)
    raw_bias, mean = reduce_over_chips(held.reshape(chips, own, -1), mean, radices, n)
    return noise_field - (jnp.tanh(raw_bias) - mean.reshape(1, -1))


def solution(mesh):
    placed = (
        P(None, "chol"),
        P("chol"),
        P(("grp", "chol"), None),
        P("grp"),
        P(("grp", "chol"), None),
    )
    return jax.shard_map(
        functools.partial(per_device, mesh.shape["chol"]),
        mesh=mesh,
        in_specs=placed,
        out_specs=P(("grp", "chol"), None),
        check_vma=False,
    )
```

```python
import functools

import jax
import jax.numpy as jnp
from jax import lax
from jax.experimental import pallas as pl
from jax.experimental.pallas import tpu as pltpu
from jax.sharding import PartitionSpec as P

F32, F16, BF16 = jnp.float32, jnp.float16, jnp.bfloat16
DIRECT_CHIPS = 8


def stage_radices(chips):
    radices = []
    while chips > 1:
        radix = 4 if chips % 4 == 0 else 2
        radices.append(radix)
        chips //= radix
    return radices


def swap(x, mask, n):
    return lax.ppermute(x, "chol", [(i, i ^ mask) for i in range(n)])


def split_kernel(greens_ref, *outs):
    me = lax.axis_index("chol")
    own = greens_ref.shape[0]
    pairs = outs[0].shape[1]
    half = outs[0].shape[0] // own
    for m in range(2 * half):
        for j in range(2):
            there = pl.multiple_of(jnp.bitwise_xor(me, 2 * m + j) * pairs, pairs)
            if m < half:
                out, at = outs[j], m
            elif m < 2 * half - 1:
                out, at = outs[2 + m - half], j
            else:
                out, at = outs[1 + half + j], 0
            out[pl.ds(at * own, own), :] = greens_ref[:, pl.ds(there, pairs)]


def split_by_device(greens, n):
    own, total = greens.shape
    pairs = total // n
    half = n // 4
    rows = [half * own] * 2 + [2 * own] * (half - 1) + [own] * 2
    outs = pl.pallas_call(
        split_kernel,
        in_specs=[pl.BlockSpec(memory_space=pltpu.VMEM)],
        out_specs=[pl.BlockSpec(memory_space=pltpu.VMEM)] * len(rows),
        out_shape=[jax.ShapeDtypeStruct((r, pairs), greens.dtype) for r in rows],
        compiler_params=pltpu.CompilerParams(vmem_limit_bytes=8 * 2**20),
        cost_estimate=pl.CostEstimate(flops=0, bytes_accessed=4 * greens.size, transcendentals=0),
    )(greens)
    return outs[0], outs[1], outs[2 : half + 1], outs[half + 1 :]


def after(x, *others):
    return lax.optimization_barrier((x,) + others)[0]


def collect_walkers(greens, n):
    own, half = greens.shape[0], n // 4
    near, other, far, last = split_by_device(greens, n)
    other = swap(other, 1, n)
    block = lambda x, i: x[i * own : (i + 1) * own]
    sent = [jnp.concatenate([block(near, i), block(other, i)]) for i in range(half)] + list(far)
    waits = {5: 1} if half == 4 else {}
    got = {0: sent[0]}
    for m in range(1, 2 * half - 1):
        message = after(sent[m], got[waits[m]]) if m in waits else sent[m]
        got[m] = swap(message, 2 * m, n)
    last = [after(x, got[w]) for x, w in zip(last, (2, 3))]
    last = [swap(x, n - 2 + j, n) for j, x in enumerate(last)]
    far = [got[m] for m in range(half, 2 * half - 1)]
    passed = [swap(jnp.concatenate([x[own:] for x in part]), 1, n) for part in (far[:1], far[1:])]
    rows = [got[m] for m in range(half)] + [x[:own] for x in far] + passed + last
    return jnp.concatenate(rows), got[1]


def place_of_source(source, n):
    half = n // 4
    far = n // 2 + (source % 2) * (half - 1) + source // 2 - half
    return jnp.where((source < n // 2) | (source >= n - 2), source, far)


def stage_kernel(parts, chol_ref, mean_ref, staged_ref, means_ref, sems):
    step = chol_ref.shape[0] // parts
    copies = []
    for t in range(parts):
        at = pl.ds(t * step, step)
        copies.append(pltpu.make_async_copy(chol_ref.at[at], staged_ref.at[at], sems.at[t]))
        copies[-1].start()
    means_ref[...] = jnp.broadcast_to(mean_ref[...], means_ref.shape)
    for copy in copies:
        copy.wait()


def stage_chol(chol, mean, parts=4):
    return pl.pallas_call(
        functools.partial(stage_kernel, parts),
        in_specs=[pl.BlockSpec(memory_space=pl.ANY), pl.BlockSpec(memory_space=pltpu.VMEM)],
        out_specs=[pl.BlockSpec(memory_space=pltpu.VMEM)] * 2,
        out_shape=[
            jax.ShapeDtypeStruct(chol.shape, chol.dtype),
            jax.ShapeDtypeStruct((16, mean.shape[1]), mean.dtype),
        ],
        scratch_shapes=[pltpu.SemaphoreType.DMA((parts,))],
        compiler_params=pltpu.CompilerParams(vmem_limit_bytes=40 * 2**20),
        cost_estimate=pl.CostEstimate(flops=0, bytes_accessed=2 * chol.size, transcendentals=0),
    )(chol, mean)


def bias_kernel(tile, index_ref, rows_ref, chol_ref, mean_ref, keep_ref, send_ref, field_ref, picked):
    half, nchol = keep_ref.shape
    walkers = rows_ref.shape[0]
    chosen = index_ref[...] == lax.broadcasted_iota(jnp.int32, (2 * half, walkers), 1)
    picked[pl.ds(0, 2 * half), :] = jnp.dot(
        chosen.astype(BF16), rows_ref[...], preferred_element_type=F32
    ).astype(BF16)
    picked[pl.ds(2 * half, 16), :] = mean_ref[...]
    for t in range(nchol // tile):
        at = pl.ds(t * tile, tile)
        part = lax.dot_general(
            picked[...], chol_ref[at, :], (((1,), (1,)), ((), ())), preferred_element_type=F32
        )
        keep_ref[:, at] = part[:half]
        send_ref[:, at] = part[half : 2 * half].astype(BF16)
        field_ref[:, at] = part[2 * half : 2 * half + 1]


def partial_bias(index, rows, chol, mean, tile):
    slots, (nchol, pairs) = index.shape[0], chol.shape
    half = slots // 2
    return pl.pallas_call(
        functools.partial(bias_kernel, tile),
        in_specs=[pl.BlockSpec(memory_space=pltpu.VMEM)] * 4,
        out_specs=[pl.BlockSpec(memory_space=pltpu.VMEM)] * 3,
        out_shape=[
            jax.ShapeDtypeStruct((half, nchol), F32),
            jax.ShapeDtypeStruct((half, nchol), BF16),
            jax.ShapeDtypeStruct((1, nchol), F32),
        ],
        scratch_shapes=[pltpu.VMEM((slots + 16, pairs), BF16)],
        compiler_params=pltpu.CompilerParams(vmem_limit_bytes=28 * 2**20),
        cost_estimate=pl.CostEstimate(
            flops=2 * slots * pairs * (nchol + rows.shape[0]),
            bytes_accessed=2 * nchol * pairs + 2 * rows.size + 6 * half * nchol,
            transcendentals=0,
        ),
    )(index, rows, chol, mean)


def swap_both(x, extra, mask, n):
    blocks, rows, g = x.shape
    extra = jnp.pad(extra[None], ((0, blocks - 1), (0, 0), (0, 0)))
    sent = jnp.concatenate([x, extra], axis=-1).astype(F16).reshape(blocks * rows, -1)
    got = swap(sent, mask, n).astype(F32).reshape(blocks, rows, -1)
    return got[..., :g], got[0, :, g:]


def reduce_over_chips(held, mean, radices, n):
    bit, mine = 1, []
    for i, radix in enumerate(radices):
        held = held.reshape((radix, held.shape[0] // radix) + held.shape[1:])
        total, mean_total = held[0], mean
        split = radix == 4 and i < len(radices) - 1
        for m in (3, 1, 2) if radix == 4 else (1,):
            skip = 1 if split and m == 3 else 0
            got, got_mean = swap_both(held[m, skip:], mean, m << bit, n)
            got = jnp.pad(got, ((skip, 0), (0, 0), (0, 0)))
            total, mean_total = total + got, mean_total + got_mean
        if split:
            mine.append(swap(held[3, 0].astype(F16), 3 << bit, n).astype(F32))
        held, mean = total, mean_total
        bit += radix.bit_length() - 1
    return held[0] + sum(mine), mean


def per_device(n, chol_vectors, mean_greens, greens, walker_order, noise_field):
    me = lax.axis_index("chol")
    own = greens.shape[0]
    chips = n // 2
    radices = stage_radices(chips)

    place = jnp.arange(n, dtype=jnp.int32)
    relative, weight, left = place // chips, 2, place % chips
    for stage, radix in enumerate(radices):
        later = 1
        for r in radices[stage + 1 :]:
            later *= r
        relative = relative + weight * (left // later)
        left, weight = left % later, weight * radix
    owners = jnp.bitwise_xor(relative, me)
    index = walker_order.reshape(n, own)[owners].reshape(-1)

    mean_row = mean_greens[None, :]
    if chips <= DIRECT_CHIPS:
        rows, ended = collect_walkers(greens, n)
        mean_row = after(mean_row, ended)
        source = jnp.bitwise_xor(index // own, me)
        index = place_of_source(source, n) * own + index % own
    else:
        rows = lax.all_to_all(greens, "chol", split_axis=1, concat_axis=0, tiled=True)
    chol, means = stage_chol(chol_vectors, mean_row)
    keep, send, mean = partial_bias(index[:, None], after(rows, means), chol, means, 512)
    mean = mean.reshape(own, -1)
    mean = mean + swap(mean, 1, n)
    held = keep + swap(send, 1, n).astype(F32)
    raw_bias, mean = reduce_over_chips(held.reshape(chips, own, -1), mean, radices, n)
    return noise_field - (jnp.tanh(raw_bias) - mean.reshape(1, -1))


def solution(mesh):
    placed = (
        P(None, "chol"),
        P("chol"),
        P(("grp", "chol"), None),
        P("grp"),
        P(("grp", "chol"), None),
    )
    return jax.shard_map(
        functools.partial(per_device, mesh.shape["chol"]),
        mesh=mesh,
        in_specs=placed,
        out_specs=P(("grp", "chol"), None),
        check_vma=False,
    )
```

```python
import functools

import jax
import jax.numpy as jnp
from jax import lax
from jax.experimental import pallas as pl
from jax.experimental.pallas import tpu as pltpu
from jax.sharding import PartitionSpec as P

F32, F16, BF16 = jnp.float32, jnp.float16, jnp.bfloat16
DIRECT_CHIPS = 8


def stage_radices(chips):
    radices = []
    while chips > 1:
        radix = 4 if chips % 4 == 0 else 2
        radices.append(radix)
        chips //= radix
    return radices


def swap(x, mask, n):
    return lax.ppermute(x, "chol", [(i, i ^ mask) for i in range(n)])


def split_kernel(greens_ref, *outs):
    me = lax.axis_index("chol")
    own = greens_ref.shape[0]
    pairs = outs[0].shape[1]
    half = outs[0].shape[0] // own
    for m in range(2 * half):
        for j in range(2):
            there = pl.multiple_of(jnp.bitwise_xor(me, 2 * m + j) * pairs, pairs)
            if m < half:
                out, at = outs[j], m
            elif m < 2 * half - 1:
                out, at = outs[2 + m - half], j
            else:
                out, at = outs[1 + half + j], 0
            out[pl.ds(at * own, own), :] = greens_ref[:, pl.ds(there, pairs)]


def split_by_device(greens, n):
    own, total = greens.shape
    pairs = total // n
    half = n // 4
    rows = [half * own] * 2 + [2 * own] * (half - 1) + [own] * 2
    outs = pl.pallas_call(
        split_kernel,
        in_specs=[pl.BlockSpec(memory_space=pltpu.VMEM)],
        out_specs=[pl.BlockSpec(memory_space=pltpu.VMEM)] * len(rows),
        out_shape=[jax.ShapeDtypeStruct((r, pairs), greens.dtype) for r in rows],
        compiler_params=pltpu.CompilerParams(vmem_limit_bytes=8 * 2**20),
        cost_estimate=pl.CostEstimate(flops=0, bytes_accessed=4 * greens.size, transcendentals=0),
    )(greens)
    return outs[0], outs[1], outs[2 : half + 1], outs[half + 1 :]


def after(x, *others):
    return lax.optimization_barrier((x,) + others)[0]


def collect_walkers(greens, n):
    own, half = greens.shape[0], n // 4
    near, other, far, last = split_by_device(greens, n)
    other = swap(other, 1, n)
    block = lambda x, i: x[i * own : (i + 1) * own]
    sent = [jnp.concatenate([block(near, i), block(other, i)]) for i in range(half)] + list(far)
    waits = {5: 1} if half == 4 else {}
    got = {0: sent[0]}
    for m in range(1, 2 * half - 1):
        message = after(sent[m], got[waits[m]]) if m in waits else sent[m]
        got[m] = swap(message, 2 * m, n)
    last = [after(x, got[w]) for x, w in zip(last, (2, 3))]
    last = [swap(x, n - 2 + j, n) for j, x in enumerate(last)]
    far = [got[m] for m in range(half, 2 * half - 1)]
    passed = [swap(jnp.concatenate([x[own:] for x in part]), 1, n) for part in (far[:1], far[1:])]
    rows = [got[m] for m in range(half)] + [x[:own] for x in far] + passed + last
    return jnp.concatenate(rows), got[1]


def place_of_source(source, n):
    half = n // 4
    far = n // 2 + (source % 2) * (half - 1) + source // 2 - half
    return jnp.where((source < n // 2) | (source >= n - 2), source, far)


def stage_kernel(parts, chol_ref, mean_ref, staged_ref, means_ref, sems):
    step = chol_ref.shape[0] // parts
    copies = []
    for t in range(parts):
        at = pl.ds(t * step, step)
        copies.append(pltpu.make_async_copy(chol_ref.at[at], staged_ref.at[at], sems.at[t]))
        copies[-1].start()
    means_ref[...] = jnp.broadcast_to(mean_ref[...], means_ref.shape)
    for copy in copies:
        copy.wait()


def stage_chol(chol, mean, parts=4):
    return pl.pallas_call(
        functools.partial(stage_kernel, parts),
        in_specs=[pl.BlockSpec(memory_space=pl.ANY), pl.BlockSpec(memory_space=pltpu.VMEM)],
        out_specs=[pl.BlockSpec(memory_space=pltpu.VMEM)] * 2,
        out_shape=[
            jax.ShapeDtypeStruct(chol.shape, chol.dtype),
            jax.ShapeDtypeStruct((16, mean.shape[1]), mean.dtype),
        ],
        scratch_shapes=[pltpu.SemaphoreType.DMA((parts,))],
        compiler_params=pltpu.CompilerParams(vmem_limit_bytes=40 * 2**20),
        cost_estimate=pl.CostEstimate(flops=0, bytes_accessed=2 * chol.size, transcendentals=0),
    )(chol, mean)


def bias_kernel(tile, index_ref, rows_ref, chol_ref, mean_ref, keep_ref, send_ref, field_ref, picked):
    half, nchol = keep_ref.shape
    walkers = rows_ref.shape[0]
    chosen = index_ref[...] == lax.broadcasted_iota(jnp.int32, (2 * half, walkers), 1)
    picked[pl.ds(0, 2 * half), :] = jnp.dot(
        chosen.astype(BF16), rows_ref[...], preferred_element_type=F32
    ).astype(BF16)
    picked[pl.ds(2 * half, 16), :] = mean_ref[...]
    for t in range(nchol // tile):
        at = pl.ds(t * tile, tile)
        part = lax.dot_general(
            picked[...], chol_ref[at, :], (((1,), (1,)), ((), ())), preferred_element_type=F32
        )
        keep_ref[:, at] = part[:half]
        send_ref[:, at] = part[half : 2 * half].astype(BF16)
        field_ref[:, at] = part[2 * half : 2 * half + 1]


def partial_bias(index, rows, chol, mean, tile):
    slots, (nchol, pairs) = index.shape[0], chol.shape
    half = slots // 2
    return pl.pallas_call(
        functools.partial(bias_kernel, tile),
        in_specs=[pl.BlockSpec(memory_space=pltpu.VMEM)] * 4,
        out_specs=[pl.BlockSpec(memory_space=pltpu.VMEM)] * 3,
        out_shape=[
            jax.ShapeDtypeStruct((half, nchol), F32),
            jax.ShapeDtypeStruct((half, nchol), BF16),
            jax.ShapeDtypeStruct((1, nchol), F32),
        ],
        scratch_shapes=[pltpu.VMEM((slots + 16, pairs), BF16)],
        compiler_params=pltpu.CompilerParams(vmem_limit_bytes=28 * 2**20),
        cost_estimate=pl.CostEstimate(
            flops=2 * slots * pairs * (nchol + rows.shape[0]),
            bytes_accessed=2 * nchol * pairs + 2 * rows.size + 6 * half * nchol,
            transcendentals=0,
        ),
    )(index, rows, chol, mean)


def swap_both(x, extra, mask, n):
    blocks, rows, g = x.shape
    extra = jnp.pad(extra[None], ((0, blocks - 1), (0, 0), (0, 0)))
    sent = jnp.concatenate([x, extra], axis=-1).astype(F16).reshape(blocks * rows, -1)
    got = swap(sent, mask, n).astype(F32).reshape(blocks, rows, -1)
    return got[..., :g], got[0, :, g:]


def reduce_over_chips(held, mean, radices, n):
    bit, mine = 1, []
    for i, radix in enumerate(radices):
        held = held.reshape((radix, held.shape[0] // radix) + held.shape[1:])
        total, mean_total = held[0], mean
        split = radix == 4 and i < len(radices) - 1
        for m in (3, 1, 2) if radix == 4 else (1,):
            skip = 1 if split and m == 3 else 0
            got, got_mean = swap_both(held[m, skip:], mean, m << bit, n)
            got = jnp.pad(got, ((skip, 0), (0, 0), (0, 0)))
            total, mean_total = total + got, mean_total + got_mean
        if split:
            mine.append(swap(held[3, 0].astype(F16), 3 << bit, n).astype(F32))
        held, mean = total, mean_total
        bit += radix.bit_length() - 1
    return held[0] + sum(mine), mean


def swap_of_four(x, q, n):
    partner = lambda i: i ^ 2 * (q if q == 3 or i % 2 == 0 else 3 - q)
    return lax.ppermute(x, "chol", [(i, partner(i)) for i in range(n)])


def reduce_over_eight(held, mean, n):
    _, own, g = held.shape
    held = held.reshape(4, 2, own, g)
    columns = lambda x, extra: jnp.concatenate([x, extra], axis=-1).astype(F16)
    none = jnp.zeros_like(mean)
    messages = (
        jnp.concatenate(
            [columns(held[1, 1], mean), columns(held[1, 0], none), columns(held[3, 0], none)]
        ),
        columns(held[2, 1], mean),
        columns(held[3, 1], mean),
    )
    messages = (messages[0],) + tuple(after(x, messages[0]) for x in messages[1:])
    first, second, third = (
        swap_of_four(x, q, n).astype(F32) for q, x in enumerate(messages, 1)
    )
    far = jnp.concatenate([held[0, 1], mean], axis=-1) + second + third + first[:own]
    across = swap(far.astype(F16), n // 2, n).astype(F32)
    passed = swap_of_four((held[2, 0] + first[2 * own :, :g]).astype(F16), 2, n).astype(F32)
    total = held[0, 0] + first[own : 2 * own, :g] + passed + across[:, :g]
    return total, far[:, g:] + across[:, g:]


def per_device(n, chol_vectors, mean_greens, greens, walker_order, noise_field):
    me = lax.axis_index("chol")
    own = greens.shape[0]
    chips = n // 2
    radices = stage_radices(chips)

    place = jnp.arange(n, dtype=jnp.int32)
    relative, weight, left = place // chips, 2, place % chips
    for stage, radix in enumerate(radices):
        later = 1
        for r in radices[stage + 1 :]:
            later *= r
        relative = relative + weight * (left // later)
        left, weight = left % later, weight * radix
    if chips == 8:
        core = jnp.bitwise_xor(place // chips, me) % 2
        four = relative // 2 % 4
        other = (core == 1) & ((four == 1) | (four == 2))
        relative = jnp.where(other, jnp.bitwise_xor(relative, 6), relative)
    owners = jnp.bitwise_xor(relative, me)
    index = walker_order.reshape(n, own)[owners].reshape(-1)

    mean_row = mean_greens[None, :]
    if chips <= DIRECT_CHIPS:
        rows, ended = collect_walkers(greens, n)
        mean_row = after(mean_row, ended)
        source = jnp.bitwise_xor(index // own, me)
        index = place_of_source(source, n) * own + index % own
    else:
        rows = lax.all_to_all(greens, "chol", split_axis=1, concat_axis=0, tiled=True)
    chol, means = stage_chol(chol_vectors, mean_row)
    keep, send, mean = partial_bias(index[:, None], after(rows, means), chol, means, 512)
    mean = mean.reshape(own, -1)
    mean = mean + swap(mean, 1, n)
    held = keep + swap(send, 1, n).astype(F32)
    held = held.reshape(chips, own, -1)
    if chips == 8:
        raw_bias, mean = reduce_over_eight(held, mean, n)
    else:
        raw_bias, mean = reduce_over_chips(held, mean, radices, n)
    return noise_field - (jnp.tanh(raw_bias) - mean.reshape(1, -1))


def solution(mesh):
    placed = (
        P(None, "chol"),
        P("chol"),
        P(("grp", "chol"), None),
        P("grp"),
        P(("grp", "chol"), None),
    )
    return jax.shard_map(
        functools.partial(per_device, mesh.shape["chol"]),
        mesh=mesh,
        in_specs=placed,
        out_specs=P(("grp", "chol"), None),
        check_vma=False,
    )
```

```python
import functools

import jax
import jax.numpy as jnp
from jax import lax
from jax.experimental import pallas as pl
from jax.experimental.pallas import tpu as pltpu
from jax.sharding import PartitionSpec as P

F32, F16, BF16 = jnp.float32, jnp.float16, jnp.bfloat16
DIRECT_CHIPS = 8


def stage_radices(chips):
    radices = []
    while chips > 1:
        radix = 4 if chips % 4 == 0 else 2
        radices.append(radix)
        chips //= radix
    return radices


def swap(x, mask, n):
    return lax.ppermute(x, "chol", [(i, i ^ mask) for i in range(n)])


def split_kernel(greens_ref, *outs):
    me = lax.axis_index("chol")
    own = greens_ref.shape[0]
    pairs = outs[0].shape[1]
    half = outs[0].shape[0] // own
    for m in range(2 * half):
        for j in range(2):
            there = pl.multiple_of(jnp.bitwise_xor(me, 2 * m + j) * pairs, pairs)
            if m < half:
                out, at = outs[j], m
            elif m < 2 * half - 1:
                out, at = outs[2 + m - half], j
            else:
                out, at = outs[1 + half + j], 0
            out[pl.ds(at * own, own), :] = greens_ref[:, pl.ds(there, pairs)]


def split_by_device(greens, n):
    own, total = greens.shape
    pairs = total // n
    half = n // 4
    rows = [half * own] * 2 + [2 * own] * (half - 1) + [own] * 2
    outs = pl.pallas_call(
        split_kernel,
        in_specs=[pl.BlockSpec(memory_space=pltpu.VMEM)],
        out_specs=[pl.BlockSpec(memory_space=pltpu.VMEM)] * len(rows),
        out_shape=[jax.ShapeDtypeStruct((r, pairs), greens.dtype) for r in rows],
        compiler_params=pltpu.CompilerParams(vmem_limit_bytes=8 * 2**20),
        cost_estimate=pl.CostEstimate(flops=0, bytes_accessed=4 * greens.size, transcendentals=0),
    )(greens)
    return outs[0], outs[1], outs[2 : half + 1], outs[half + 1 :]


def after(x, *others):
    return lax.optimization_barrier((x,) + others)[0]


def collect_walkers(greens, n):
    own, half = greens.shape[0], n // 4
    near, other, far, last = split_by_device(greens, n)
    other = swap(other, 1, n)
    block = lambda x, i: x[i * own : (i + 1) * own]
    sent = [jnp.concatenate([block(near, i), block(other, i)]) for i in range(half)] + list(far)
    waits = {5: 1} if half == 4 else {}
    got = {0: sent[0]}
    for m in range(1, 2 * half - 1):
        message = after(sent[m], got[waits[m]]) if m in waits else sent[m]
        got[m] = swap(message, 2 * m, n)
    last = [after(x, got[w]) for x, w in zip(last, (2, 3))]
    last = [swap(x, n - 2 + j, n) for j, x in enumerate(last)]
    far = [got[m] for first in (0, 1) for m in range(half + first, 2 * half - 1, 2)]
    early = half // 2
    passed = [swap(jnp.concatenate([x[own:] for x in part]), 1, n) for part in (far[:early], far[early:])]
    rows = [got[m] for m in range(half)] + [x[:own] for x in far] + passed + last
    return jnp.concatenate(rows), got[1]


def place_of_source(source, n):
    half = n // 4
    chip = source // 2 - half
    far = n // 2 + (source % 2) * (half - 1) + chip % 2 * (half // 2) + chip // 2
    return jnp.where((source < n // 2) | (source >= n - 2), source, far)


def stage_kernel(parts, chol_ref, mean_ref, staged_ref, means_ref, sems):
    step = chol_ref.shape[0] // parts
    copies = []
    for t in range(parts):
        at = pl.ds(t * step, step)
        copies.append(pltpu.make_async_copy(chol_ref.at[at], staged_ref.at[at], sems.at[t]))
        copies[-1].start()
    means_ref[...] = jnp.broadcast_to(mean_ref[...], means_ref.shape)
    for copy in copies:
        copy.wait()


def stage_chol(chol, mean, parts=4):
    return pl.pallas_call(
        functools.partial(stage_kernel, parts),
        in_specs=[pl.BlockSpec(memory_space=pl.ANY), pl.BlockSpec(memory_space=pltpu.VMEM)],
        out_specs=[pl.BlockSpec(memory_space=pltpu.VMEM)] * 2,
        out_shape=[
            jax.ShapeDtypeStruct(chol.shape, chol.dtype),
            jax.ShapeDtypeStruct((16, mean.shape[1]), mean.dtype),
        ],
        scratch_shapes=[pltpu.SemaphoreType.DMA((parts,))],
        compiler_params=pltpu.CompilerParams(vmem_limit_bytes=40 * 2**20),
        cost_estimate=pl.CostEstimate(flops=0, bytes_accessed=2 * chol.size, transcendentals=0),
    )(chol, mean)


def bias_kernel(tile, index_ref, rows_ref, chol_ref, mean_ref, keep_ref, send_ref, field_ref, picked):
    half, nchol = keep_ref.shape
    walkers = rows_ref.shape[0]
    chosen = index_ref[...] == lax.broadcasted_iota(jnp.int32, (2 * half, walkers), 1)
    picked[pl.ds(0, 2 * half), :] = jnp.dot(
        chosen.astype(BF16), rows_ref[...], preferred_element_type=F32
    ).astype(BF16)
    picked[pl.ds(2 * half, 16), :] = mean_ref[...]
    for t in range(nchol // tile):
        at = pl.ds(t * tile, tile)
        part = lax.dot_general(
            picked[...], chol_ref[at, :], (((1,), (1,)), ((), ())), preferred_element_type=F32
        )
        keep_ref[:, at] = part[:half]
        send_ref[:, at] = part[half : 2 * half].astype(BF16)
        field_ref[:, at] = part[2 * half : 2 * half + 1]


def partial_bias(index, rows, chol, mean, tile):
    slots, (nchol, pairs) = index.shape[0], chol.shape
    half = slots // 2
    return pl.pallas_call(
        functools.partial(bias_kernel, tile),
        in_specs=[pl.BlockSpec(memory_space=pltpu.VMEM)] * 4,
        out_specs=[pl.BlockSpec(memory_space=pltpu.VMEM)] * 3,
        out_shape=[
            jax.ShapeDtypeStruct((half, nchol), F32),
            jax.ShapeDtypeStruct((half, nchol), BF16),
            jax.ShapeDtypeStruct((1, nchol), F32),
        ],
        scratch_shapes=[pltpu.VMEM((slots + 16, pairs), BF16)],
        compiler_params=pltpu.CompilerParams(vmem_limit_bytes=28 * 2**20),
        cost_estimate=pl.CostEstimate(
            flops=2 * slots * pairs * (nchol + rows.shape[0]),
            bytes_accessed=2 * nchol * pairs + 2 * rows.size + 6 * half * nchol,
            transcendentals=0,
        ),
    )(index, rows, chol, mean)


def swap_both(x, extra, mask, n):
    blocks, rows, g = x.shape
    extra = jnp.pad(extra[None], ((0, blocks - 1), (0, 0), (0, 0)))
    sent = jnp.concatenate([x, extra], axis=-1).astype(F16).reshape(blocks * rows, -1)
    got = swap(sent, mask, n).astype(F32).reshape(blocks, rows, -1)
    return got[..., :g], got[0, :, g:]


def reduce_over_chips(held, mean, radices, n):
    bit, mine = 1, []
    for i, radix in enumerate(radices):
        held = held.reshape((radix, held.shape[0] // radix) + held.shape[1:])
        total, mean_total = held[0], mean
        split = radix == 4 and i < len(radices) - 1
        for m in (3, 1, 2) if radix == 4 else (1,):
            skip = 1 if split and m == 3 else 0
            got, got_mean = swap_both(held[m, skip:], mean, m << bit, n)
            got = jnp.pad(got, ((skip, 0), (0, 0), (0, 0)))
            total, mean_total = total + got, mean_total + got_mean
        if split:
            mine.append(swap(held[3, 0].astype(F16), 3 << bit, n).astype(F32))
        held, mean = total, mean_total
        bit += radix.bit_length() - 1
    return held[0] + sum(mine), mean


def swap_of_four(x, q, n):
    partner = lambda i: i ^ 2 * (q if q == 3 or i % 2 == 0 else 3 - q)
    return lax.ppermute(x, "chol", [(i, partner(i)) for i in range(n)])


def reduce_over_eight(held, mean, n):
    _, own, g = held.shape
    held = held.reshape(4, 2, own, g)
    columns = lambda x, extra: jnp.concatenate([x, extra], axis=-1).astype(F16)
    none = jnp.zeros_like(mean)
    messages = (
        jnp.concatenate(
            [columns(held[1, 1], mean), columns(held[1, 0], none), columns(held[3, 0], none)]
        ),
        columns(held[2, 1], mean),
        columns(held[3, 1], mean),
    )
    messages = (messages[0],) + tuple(after(x, messages[0]) for x in messages[1:])
    first, second, third = (
        swap_of_four(x, q, n).astype(F32) for q, x in enumerate(messages, 1)
    )
    far = jnp.concatenate([held[0, 1], mean], axis=-1) + second + third + first[:own]
    across = swap(far.astype(F16), n // 2, n).astype(F32)
    passed = swap_of_four((held[2, 0] + first[2 * own :, :g]).astype(F16), 2, n).astype(F32)
    total = held[0, 0] + first[own : 2 * own, :g] + passed + across[:, :g]
    return total, far[:, g:] + across[:, g:]


def per_device(n, chol_vectors, mean_greens, greens, walker_order, noise_field):
    me = lax.axis_index("chol")
    own = greens.shape[0]
    chips = n // 2
    radices = stage_radices(chips)

    place = jnp.arange(n, dtype=jnp.int32)
    relative, weight, left = place // chips, 2, place % chips
    for stage, radix in enumerate(radices):
        later = 1
        for r in radices[stage + 1 :]:
            later *= r
        relative = relative + weight * (left // later)
        left, weight = left % later, weight * radix
    if chips == 8:
        core = jnp.bitwise_xor(place // chips, me) % 2
        four = relative // 2 % 4
        other = (core == 1) & ((four == 1) | (four == 2))
        relative = jnp.where(other, jnp.bitwise_xor(relative, 6), relative)
    owners = jnp.bitwise_xor(relative, me)
    index = walker_order.reshape(n, own)[owners].reshape(-1)

    mean_row = mean_greens[None, :]
    if chips <= DIRECT_CHIPS:
        rows, ended = collect_walkers(greens, n)
        mean_row = after(mean_row, ended)
        source = jnp.bitwise_xor(index // own, me)
        index = place_of_source(source, n) * own + index % own
    else:
        rows = lax.all_to_all(greens, "chol", split_axis=1, concat_axis=0, tiled=True)
    chol, means = stage_chol(chol_vectors, mean_row)
    keep, send, mean = partial_bias(index[:, None], after(rows, means), chol, means, 512)
    mean = mean.reshape(own, -1)
    mean = mean + swap(mean, 1, n)
    held = keep + swap(send, 1, n).astype(F32)
    held = held.reshape(chips, own, -1)
    if chips == 8:
        raw_bias, mean = reduce_over_eight(held, mean, n)
    else:
        raw_bias, mean = reduce_over_chips(held, mean, radices, n)
    return noise_field - (jnp.tanh(raw_bias) - mean.reshape(1, -1))


def solution(mesh):
    placed = (
        P(None, "chol"),
        P("chol"),
        P(("grp", "chol"), None),
        P("grp"),
        P(("grp", "chol"), None),
    )
    return jax.shard_map(
        functools.partial(per_device, mesh.shape["chol"]),
        mesh=mesh,
        in_specs=placed,
        out_specs=P(("grp", "chol"), None),
        check_vma=False,
    )
```

```python
import functools

import jax
import jax.numpy as jnp
from jax import lax
from jax.experimental import pallas as pl
from jax.experimental.pallas import tpu as pltpu
from jax.sharding import PartitionSpec as P

F32, F16, BF16 = jnp.float32, jnp.float16, jnp.bfloat16
DIRECT_CHIPS = 8


def stage_radices(chips):
    radices = []
    while chips > 1:
        radix = 4 if chips % 4 == 0 else 2
        radices.append(radix)
        chips //= radix
    return radices


def swap(x, mask, n):
    return lax.ppermute(x, "chol", [(i, i ^ mask) for i in range(n)])


def split_kernel(greens_ref, *outs):
    me = lax.axis_index("chol")
    own = greens_ref.shape[0]
    pairs = outs[0].shape[1]
    half = outs[0].shape[0] // own
    for m in range(2 * half):
        for j in range(2):
            there = pl.multiple_of(jnp.bitwise_xor(me, 2 * m + j) * pairs, pairs)
            if m < half:
                out, at = outs[j], m
            elif m < 2 * half - 1:
                out, at = outs[2 + m - half], j
            else:
                out, at = outs[1 + half + j], 0
            out[pl.ds(at * own, own), :] = greens_ref[:, pl.ds(there, pairs)]


def split_by_device(greens, n):
    own, total = greens.shape
    pairs = total // n
    half = n // 4
    rows = [half * own] * 2 + [2 * own] * (half - 1) + [own] * 2
    outs = pl.pallas_call(
        split_kernel,
        in_specs=[pl.BlockSpec(memory_space=pltpu.VMEM)],
        out_specs=[pl.BlockSpec(memory_space=pltpu.VMEM)] * len(rows),
        out_shape=[jax.ShapeDtypeStruct((r, pairs), greens.dtype) for r in rows],
        compiler_params=pltpu.CompilerParams(vmem_limit_bytes=8 * 2**20),
        cost_estimate=pl.CostEstimate(flops=0, bytes_accessed=4 * greens.size, transcendentals=0),
    )(greens)
    return outs[0], outs[1], outs[2 : half + 1], outs[half + 1 :]


def after(x, *others):
    return lax.optimization_barrier((x,) + others)[0]


def collect_walkers(greens, n):
    own, half = greens.shape[0], n // 4
    near, other, far, last = split_by_device(greens, n)
    other = swap(other, 1, n)
    block = lambda x, i: x[i * own : (i + 1) * own]
    sent = [jnp.concatenate([block(near, i), block(other, i)]) for i in range(half)] + list(far)
    waits = {5: 1} if half == 4 else {}
    got = {0: sent[0]}
    for m in range(1, 2 * half - 1):
        message = after(sent[m], got[waits[m]]) if m in waits else sent[m]
        got[m] = swap(message, 2 * m, n)
    last = [after(x, got[w]) for x, w in zip(last, (2, 3))]
    last = [swap(x, n - 2 + j, n) for j, x in enumerate(last)]
    far = [got[m] for m in range(half, 2 * half - 1)]
    passed = [swap(jnp.concatenate([x[own:] for x in part]), 1, n) for part in (far[:1], far[1:])]
    rows = [got[m] for m in range(half)] + [x[:own] for x in far] + passed + last
    return jnp.concatenate(rows), got[1]


def place_of_source(source, n):
    half = n // 4
    far = n // 2 + (source % 2) * (half - 1) + source // 2 - half
    return jnp.where((source < n // 2) | (source >= n - 2), source, far)


def stage_kernel(parts, chol_ref, mean_ref, staged_ref, means_ref, sems):
    step = chol_ref.shape[0] // parts
    copies = []
    for t in range(parts):
        at = pl.ds(t * step, step)
        copies.append(pltpu.make_async_copy(chol_ref.at[at], staged_ref.at[at], sems.at[t]))
        copies[-1].start()
    means_ref[...] = jnp.broadcast_to(mean_ref[...], means_ref.shape)
    for copy in copies:
        copy.wait()


def stage_chol(chol, mean, parts=4):
    return pl.pallas_call(
        functools.partial(stage_kernel, parts),
        in_specs=[pl.BlockSpec(memory_space=pl.ANY), pl.BlockSpec(memory_space=pltpu.VMEM)],
        out_specs=[pl.BlockSpec(memory_space=pltpu.VMEM)] * 2,
        out_shape=[
            jax.ShapeDtypeStruct(chol.shape, chol.dtype),
            jax.ShapeDtypeStruct((16, mean.shape[1]), mean.dtype),
        ],
        scratch_shapes=[pltpu.SemaphoreType.DMA((parts,))],
        compiler_params=pltpu.CompilerParams(vmem_limit_bytes=40 * 2**20),
        cost_estimate=pl.CostEstimate(flops=0, bytes_accessed=2 * chol.size, transcendentals=0),
    )(chol, mean)


def bias_kernel(tile, index_ref, rows_ref, chol_ref, mean_ref, keep_ref, send_ref, field_ref, picked):
    half, nchol = keep_ref.shape
    walkers = rows_ref.shape[0]
    chosen = index_ref[...] == lax.broadcasted_iota(jnp.int32, (2 * half, walkers), 1)
    picked[pl.ds(0, 2 * half), :] = jnp.dot(
        chosen.astype(BF16), rows_ref[...], preferred_element_type=F32
    ).astype(BF16)
    picked[pl.ds(2 * half, 16), :] = mean_ref[...]
    for t in range(nchol // tile):
        at = pl.ds(t * tile, tile)
        part = lax.dot_general(
            picked[...], chol_ref[at, :], (((1,), (1,)), ((), ())), preferred_element_type=F32
        )
        keep_ref[:, at] = part[:half]
        send_ref[:, at] = part[half : 2 * half].astype(BF16)
        field_ref[:, at] = part[2 * half : 2 * half + 1]


def partial_bias(index, rows, chol, mean, tile):
    slots, (nchol, pairs) = index.shape[0], chol.shape
    half = slots // 2
    return pl.pallas_call(
        functools.partial(bias_kernel, tile),
        in_specs=[pl.BlockSpec(memory_space=pltpu.VMEM)] * 4,
        out_specs=[pl.BlockSpec(memory_space=pltpu.VMEM)] * 3,
        out_shape=[
            jax.ShapeDtypeStruct((half, nchol), F32),
            jax.ShapeDtypeStruct((half, nchol), BF16),
            jax.ShapeDtypeStruct((1, nchol), F32),
        ],
        scratch_shapes=[pltpu.VMEM((slots + 16, pairs), BF16)],
        compiler_params=pltpu.CompilerParams(vmem_limit_bytes=28 * 2**20),
        cost_estimate=pl.CostEstimate(
            flops=2 * slots * pairs * (nchol + rows.shape[0]),
            bytes_accessed=2 * nchol * pairs + 2 * rows.size + 6 * half * nchol,
            transcendentals=0,
        ),
    )(index, rows, chol, mean)


def swap_both(x, extra, mask, n):
    blocks, rows, g = x.shape
    extra = jnp.pad(extra[None], ((0, blocks - 1), (0, 0), (0, 0)))
    sent = jnp.concatenate([x, extra], axis=-1).astype(F16).reshape(blocks * rows, -1)
    got = swap(sent, mask, n).astype(F32).reshape(blocks, rows, -1)
    return got[..., :g], got[0, :, g:]


def reduce_over_chips(held, mean, radices, n):
    bit, mine = 1, []
    for i, radix in enumerate(radices):
        held = held.reshape((radix, held.shape[0] // radix) + held.shape[1:])
        total, mean_total = held[0], mean
        split = radix == 4 and i < len(radices) - 1
        for m in (3, 1, 2) if radix == 4 else (1,):
            skip = 1 if split and m == 3 else 0
            got, got_mean = swap_both(held[m, skip:], mean, m << bit, n)
            got = jnp.pad(got, ((skip, 0), (0, 0), (0, 0)))
            total, mean_total = total + got, mean_total + got_mean
        if split:
            mine.append(swap(held[3, 0].astype(F16), 3 << bit, n).astype(F32))
        held, mean = total, mean_total
        bit += radix.bit_length() - 1
    return held[0] + sum(mine), mean


def swap_of_four(x, q, n):
    partner = lambda i: i ^ 2 * (q if q == 3 or i % 2 == 0 else 3 - q)
    return lax.ppermute(x, "chol", [(i, partner(i)) for i in range(n)])


def reduce_over_eight(held, mean, n):
    _, own, g = held.shape
    held = held.reshape(4, 2, own, g)
    columns = lambda x, extra: jnp.concatenate([x, extra], axis=-1).astype(F16)
    none = jnp.zeros_like(mean)
    messages = (
        jnp.concatenate(
            [columns(held[1, 1], mean), columns(held[1, 0], none), columns(held[3, 0], none)]
        ),
        columns(held[2, 1], mean),
        columns(held[3, 1], mean),
    )
    messages = (messages[0],) + tuple(after(x, messages[0]) for x in messages[1:])
    first, second, third = (
        swap_of_four(x, q, n).astype(F32) for q, x in enumerate(messages, 1)
    )
    far = jnp.concatenate([held[0, 1], mean], axis=-1) + second + third + first[:own]
    across = swap(far.astype(F16), n // 2, n).astype(F32)
    passed = swap_of_four((held[2, 0] + first[2 * own :, :g]).astype(F16), 2, n).astype(F32)
    total = held[0, 0] + first[own : 2 * own, :g] + passed + across[:, :g]
    return total, far[:, g:] + across[:, g:]


def per_device(n, chol_vectors, mean_greens, greens, walker_order, noise_field):
    me = lax.axis_index("chol")
    own = greens.shape[0]
    chips = n // 2
    radices = stage_radices(chips)

    mean_row = mean_greens[None, :]
    if chips <= DIRECT_CHIPS:
        rows, ended = collect_walkers(greens, n)
        mean_row = after(mean_row, ended)
        walker_order = after(walker_order, ended)
    else:
        rows = lax.all_to_all(greens, "chol", split_axis=1, concat_axis=0, tiled=True)
    place = jnp.arange(n, dtype=jnp.int32)
    relative, weight, left = place // chips, 2, place % chips
    for stage, radix in enumerate(radices):
        later = 1
        for r in radices[stage + 1 :]:
            later *= r
        relative = relative + weight * (left // later)
        left, weight = left % later, weight * radix
    if chips == 8:
        core = jnp.bitwise_xor(place // chips, me) % 2
        four = relative // 2 % 4
        other = (core == 1) & ((four == 1) | (four == 2))
        relative = jnp.where(other, jnp.bitwise_xor(relative, 6), relative)
    owners = jnp.bitwise_xor(relative, me)
    index = walker_order.reshape(n, own)[owners].reshape(-1)
    if chips <= DIRECT_CHIPS:
        source = jnp.bitwise_xor(index // own, me)
        index = place_of_source(source, n) * own + index % own
    chol, means = stage_chol(chol_vectors, mean_row)
    keep, send, mean = partial_bias(index[:, None], after(rows, means), chol, means, 512)
    mean = mean.reshape(own, -1)
    mean = mean + swap(mean, 1, n)
    held = keep + swap(send, 1, n).astype(F32)
    held = held.reshape(chips, own, -1)
    if chips == 8:
        raw_bias, mean = reduce_over_eight(held, mean, n)
    else:
        raw_bias, mean = reduce_over_chips(held, mean, radices, n)
    return noise_field - (jnp.tanh(raw_bias) - mean.reshape(1, -1))


def solution(mesh):
    placed = (
        P(None, "chol"),
        P("chol"),
        P(("grp", "chol"), None),
        P("grp"),
        P(("grp", "chol"), None),
    )
    return jax.shard_map(
        functools.partial(per_device, mesh.shape["chol"]),
        mesh=mesh,
        in_specs=placed,
        out_specs=P(("grp", "chol"), None),
        check_vma=False,
    )
```
